256 devices in a mesh: lat: 8 (over y_hi, x), lon: 32 (over y_lo, z, core).
Axes of the slice: x: 4, y: 4 (y_hi: 2, y_lo: 2; y = y_hi * 2 + y_lo), z: 8, core: 2. Of those that a mesh axis runs over, the one named last changes fastest.
Arguments:
- noise: float32 [2, 16, 512, 4096], P(None, None, 'lat', 'lon'), may hold values from -6 to 6
- land_mask: int32 [16, 512, 4096], P(None, 'lat', 'lon'), may hold values from 0 to 1, as said below
- east_coef: float32 [16, 512, 4096], P(None, 'lat', 'lon'), may hold values from 0 to 0.24, as said below
- north_coef: float32 [16, 512, 4096], P(None, 'lat', 'lon'), may hold values from 0 to 0.24, as said below
Outputs:
- state_field: float32 [2, 16, 512, 4096], P(None, None, 'lat', 'lon')
The draws below stay inside these ranges and needn't reach their ends.
Inputs may be any that keep to these rules, and one draw needn't show every extreme that they name: `land_mask`: 1 marks ocean; a cell that is ocean at a level is ocean at every shallower level; along the top row the mask at column j equals that at column 4095 - j. `east_coef`: zero on every face with land on either side (the top row's northern face joins column j to column 4095 - j). `north_coef`: zero on every face with land on either side (the top row's northern face joins column j to column 4095 - j).
All inputs are finite; a program needn't handle non-finite values.
Results may differ from the reference program's by a relative error of at most 0.00002.
Values sent between devices are 32-bit elements; how exact they have to be, the bound alone decides.
No kernel may reach another device: no remote copies, remote signals or barrier semaphores. Data moves between devices by JAX's collectives and lax.ppermute only.
A program may use at most 64 MiB of HBM per device.

```python
import jax
import jax.numpy as jnp

MEMBERS = 2
LEVELS = 16
ITERS = 2
NLAT = 512
NLON = 4096


def ocean_levels(key):
    depth_levels = jax.random.randint(jax.random.fold_in(key, 101), (NLAT, NLON), 0, 3 * LEVELS // 2 + 1)
    column_ids = jnp.arange(NLON, dtype=jnp.int32)
    mirror_ids = jnp.where(column_ids < NLON // 2, column_ids, NLON - 1 - column_ids)
    top_depths = depth_levels[NLAT - 1][mirror_ids]
    depth_levels = depth_levels.at[NLAT - 1].set(top_depths)
    level_ids = jnp.arange(LEVELS, dtype=jnp.int32)[:, None, None]
    return jnp.where(level_ids < depth_levels[None, :, :], 1, 0).astype(jnp.int32)


def coef_values(key):
    low = jnp.log(jnp.float32(0.02))
    high = jnp.log(jnp.float32(0.24))
    return jnp.exp(jax.random.uniform(key, (LEVELS, NLAT, NLON), jnp.float32, low, high))


def draw_land_mask(key, part):
    return ocean_levels(key)


def draw_east_coef(key, part):
    ocean_mask = ocean_levels(key).astype(jnp.float32)
    key = jax.random.fold_in(key, 7)
    face_open = ocean_mask * jnp.roll(ocean_mask, -1, axis=2)
    return (coef_values(key) * face_open).astype(jnp.float32)


def draw_north_coef(key, part):
    ocean_mask = ocean_levels(key).astype(jnp.float32)
    key = jax.random.fold_in(key, 11)
    above = jnp.concatenate([ocean_mask[:, 1:, :], jnp.flip(ocean_mask[:, -1:, :], axis=2)], axis=1)
    face_open = ocean_mask * above
    return (coef_values(key) * face_open).astype(jnp.float32)


def shard_levels(own_key, shape, shards, low, largest):
    level = 1.0
    for dim, parts in shards:
        steps = jax.random.uniform(jax.random.fold_in(jax.random.fold_in(own_key, 6), dim), (parts,), jnp.float32, low / len(shards), largest / len(shards))
        level = level * jnp.repeat(jnp.exp(steps), shape[dim] // parts).reshape((-1,) + (1,) * (len(shape) - 1 - dim))
    return level


def gaussian(rng, extent, deviation, reach, split=(), kind=jnp.bfloat16):
    gain = shard_levels(rng, extent, split, -0.22, 0.18) if split else 1.0
    array = jax.random.normal(rng, extent, jnp.float32) * deviation * gain
    return jnp.minimum(jnp.maximum(array, -reach), reach).astype(kind)


def setup_inputs(seed: int = 0) -> dict:
    streams_of = jax.random.split(jax.random.key(seed), 5)
    return {
        "noise": gaussian(streams_of[0], (MEMBERS, LEVELS, NLAT, NLON), 1.0, 6.0, ((2, 8), (3, 32)), jnp.float32),
        "land_mask": draw_land_mask(jax.random.fold_in(streams_of[4], 71), 0),
        "east_coef": draw_east_coef(jax.random.fold_in(streams_of[4], 71), 0),
        "north_coef": draw_north_coef(jax.random.fold_in(streams_of[4], 71), 0),
    }


def reference(noise, land_mask, east_coef, north_coef):
    ocean_mask = land_mask.astype(jnp.float32)
    west_coef = jnp.roll(east_coef, 1, axis=2)
    south_coef = jnp.concatenate([jnp.zeros_like(north_coef[:, :1, :]), north_coef[:, :-1, :]], axis=1)
    state_field = noise * ocean_mask
    for iteration in range(ITERS):
        east_vals = jnp.roll(state_field, -1, axis=3)
        west_vals = jnp.roll(state_field, 1, axis=3)
        north_vals = jnp.concatenate([state_field[:, :, 1:, :], jnp.flip(state_field[:, :, -1:, :], axis=3)], axis=2)
        south_vals = jnp.concatenate([jnp.zeros_like(state_field[:, :, :1, :]), state_field[:, :, :-1, :]], axis=2)
        net_flux = east_coef * (east_vals - state_field) - west_coef * (state_field - west_vals)
        net_flux = net_flux + north_coef * (north_vals - state_field) - south_coef * (state_field - south_vals)
        state_field = ocean_mask * (state_field + net_flux)
    return state_field
```

```python
import jax
import jax.numpy as jnp
from jax import lax
from jax.experimental import pallas as pl
from jax.experimental.pallas import tpu as pltpu
from jax.sharding import PartitionSpec as P


LEVELS, ROWS, COLS = 16, 64, 128
PACKED = 72
F32 = jnp.float32
VMEM = pl.BlockSpec(memory_space=pltpu.VMEM)


def lanes(rows):
    return lax.broadcasted_iota(jnp.int32, (rows, COLS), 1)


def turned(x, shift):
    return pltpu.roll(x, shift % COLS if isinstance(shift, int) else shift, 1)


def edge_rows(noise_lo, noise_hi, mask_lo, mask_hi, east_lo, east_hi, north_lo, north_hi, out_b, out_a):
    lat = lax.axis_index("lat")
    top_block = lat == lax.axis_size("lat") - 1
    even = lax.rem(lat, 2) == 0
    lane = lanes(LEVELS)

    def lateral(u, east, west):
        return east * (turned(u, -1) - u) - west * (u - turned(u, 1))

    def inner_faces(east):
        return jnp.where(lane == COLS - 1, 0.0, east), jnp.where(lane == 0, 0.0, turned(east, 1))

    mask_t = mask_hi[:, 7, :].astype(F32)
    mask_t2 = mask_hi[:, 6, :].astype(F32)
    mask_b = mask_lo[:, 0, :].astype(F32)
    mask_b2 = mask_lo[:, 1, :].astype(F32)
    east_t, west_t = inner_faces(east_hi[:, 7, :])
    east_b, west_b = inner_faces(east_lo[:, 0, :])
    south_t = north_hi[:, 6, :]
    north_b = north_lo[:, 0, :]
    top, bottom = [], []
    top_p, bottom_p = [], []
    for m in range(2):
        u = noise_hi[m, :, 7, :] * mask_t
        v = noise_hi[m, :, 6, :] * mask_t2
        top.append(u)
        top_p.append(mask_t * (u + lateral(u, east_t, west_t) - south_t * (u - v)))
        u = noise_lo[m, :, 0, :] * mask_b
        v = noise_lo[m, :, 1, :] * mask_b2
        bottom.append(u)
        bottom_p.append(mask_b * (u + lateral(u, east_b, west_b) + north_b * (v - u)))
    top += top_p + [north_hi[:, 7, :] * mask_t, east_hi[:, 7, :] * mask_t]
    bottom += bottom_p + [mask_b, east_lo[:, 0, :] * mask_b]
    flip = jnp.where(top_block, COLS - 1 - lane, lane)
    for q in range(6):
        rows = pl.ds(q * LEVELS, LEVELS)
        out_b[rows, :] = jnp.where(even, top[q], bottom[q])
        crossed = jnp.take_along_axis(top[q], flip, axis=1)
        out_a[rows, :] = jnp.where(even, bottom[q], crossed)


def first_step(noise, mask, east, north, out_u, out_pairs, out_faces):
    lane = lanes(ROWS)
    row = lax.broadcasted_iota(jnp.int32, (ROWS, COLS), 0)
    pair = lane // 2

    def level(l, carry):
        pairs, faces = carry
        k = mask[l].astype(F32)
        e_all = east[l]
        n_all = north[l]
        e = jnp.where(lane == COLS - 1, 0.0, e_all)
        w = jnp.where(lane == 0, 0.0, turned(e_all, 1))
        n = jnp.where(row == ROWS - 1, 0.0, n_all)
        s = jnp.where(row == 0, 0.0, pltpu.roll(n_all, 1, 0))
        edge = jnp.where(lane == COLS - 1, e_all * k, k)
        faces = jnp.where(pair == l, turned(edge, 2 * l + 1), faces)
        for m in range(2):
            u = noise[m, l] * k
            flux = e * (turned(u, -1) - u) - w * (u - turned(u, 1))
            flux = flux + n * (pltpu.roll(u, ROWS - 1, 0) - u) - s * (u - pltpu.roll(u, 1, 0))
            v = k * (u + flux)
            out_u[m, l] = v
            pairs = jnp.where(pair == m * 16 + l, turned(u, m * 32 + 2 * l + 1), pairs)
            pairs = jnp.where(pair == 32 + m * 16 + l, turned(v, 64 + m * 32 + 2 * l + 1), pairs)
        return pairs, faces

    zero = jnp.zeros((ROWS, COLS), F32)
    pairs, faces = lax.fori_loop(0, LEVELS, level, (zero, zero))
    out_pairs[...] = pairs
    out_faces[...] = faces


def join_rows(
    own_b, own_a, got_b, got_a, pairs, faces, send_1, send_2, out_pairs, out_faces, out_rows, south, north, side
):
    lat = lax.axis_index("lat")
    top_block = lat == lax.axis_size("lat") - 1
    even = lax.rem(lat, 2) == 0
    even_lon = lax.rem(lax.axis_index("lon"), 2) == 0

    def part(q):
        rows = pl.ds(q * LEVELS, LEVELS)
        ob, oa, gb, ga = own_b[rows, :], own_a[rows, :], got_b[rows, :], got_a[rows, :]
        return ob, oa, jnp.where(even, gb, ga), jnp.where(even, ga, gb)

    flip = COLS - 1 - lanes(LEVELS)

    def own(q):
        ob, oa, _, _ = part(q)
        back = jnp.where(top_block, jnp.take_along_axis(oa, flip, axis=1), oa)
        return jnp.where(even, ob, back), jnp.where(even, oa, ob)

    def put(ref, q, x):
        ref[pl.ds(q * 32, LEVELS, stride=2), :] = x
        ref[pl.ds(q * 32 + 1, LEVELS, stride=2), :] = x

    own_n, own_k = own(4)
    _, _, far_n, far_s = part(4)
    ghost_n = jnp.where(top_block, far_n, own_n * far_n)
    for m in range(2):
        own_t, own_bot = own(m)
        _, _, up, down = part(m)
        _, _, up_p, down_p = part(2 + m)
        gain_s = own_k * far_s * (down - own_bot)
        gain_n = own_n * (up - own_t)
        out_rows[pl.ds(m * LEVELS, LEVELS), :] = gain_s
        out_rows[pl.ds((2 + m) * LEVELS, LEVELS), :] = gain_n
        out_rows[pl.ds((4 + m) * LEVELS, LEVELS), :] = down_p - far_s * (down - own_bot)
        out_rows[pl.ds((6 + m) * LEVELS, LEVELS), :] = up_p - ghost_n * (up - own_t)
        put(south, m, down)
        put(south, 2 + m, gain_s)
        put(north, m, up)
        put(north, 2 + m, gain_n)
    out_rows[pl.ds(8 * LEVELS, LEVELS), :] = far_s
    _, _, up_e, down_e = part(5)
    put(side, 0, down_e)
    put(side, 1, up_e)
    put(side, 2, up_e)
    put(side, 3, up_e)

    lane1 = lanes(1)
    odd1 = lax.rem(lane1, 2) == 1
    turned_s = jnp.transpose(south[...])
    turned_n = jnp.transpose(north[...])
    turned_e = jnp.transpose(side[...])
    row_s = jnp.where(odd1, turned_s[0:1, :], turned_s[COLS - 1 : COLS, :])
    row_n = jnp.where(odd1, turned_n[0:1, :], turned_n[COLS - 1 : COLS, :])
    gain = lane1 >= 64
    out_pairs[0:ROWS, :] = pairs[...]
    out_pairs[0:1, :] = pairs[0:1, :] + jnp.where(gain, row_s, 0.0)
    out_pairs[ROWS - 1 : ROWS, :] = pairs[ROWS - 1 : ROWS, :] + jnp.where(gain, row_n, 0.0)
    out_pairs[ROWS:PACKED, :] = jnp.zeros((PACKED - ROWS, COLS), F32)
    out_pairs[ROWS : ROWS + 1, :] = row_s
    out_pairs[ROWS + 1 : ROWS + 2, :] = row_n
    face_s = jnp.where(odd1, 1.0, turned_e[COLS - 1 : COLS, :])
    near = turned(turned_e[COLS - 1 : COLS, :], -32)
    mirrored = turned(turned_e[0:1, :], -32)
    face_n = jnp.where(
        top_block, jnp.where(odd1, mirrored, 1.0), jnp.where(odd1, 1.0, near)
    )
    out_faces[0:ROWS, :] = faces[...]
    out_faces[ROWS:PACKED, :] = jnp.zeros((PACKED - ROWS, COLS), F32)
    out_faces[ROWS : ROWS + 1, :] = face_s
    out_faces[ROWS + 1 : ROWS + 2, :] = face_n
    all_pairs = out_pairs[...]
    all_faces = out_faces[...]
    odd = lax.rem(lanes(PACKED), 2) == 1
    eastward = jnp.where(odd, turned(all_pairs, 1), all_faces)
    westward = jnp.where(odd, all_faces, turned(all_pairs, -1))
    send_1[...] = jnp.where(even_lon, eastward, westward)
    send_2[...] = jnp.where(even_lon, westward, eastward)


def second_step(
    u1, mask, east, north, got_1, got_2, pairs, faces, rows, out, edge_u, edge_g, edge_c, held, sem
):
    even_lon = lax.rem(lax.axis_index("lon"), 2) == 0
    lane72 = lanes(PACKED)
    row72 = lax.broadcasted_iota(jnp.int32, (PACKED, COLS), 0)
    odd = lax.rem(lane72, 2) == 1
    from_east = jnp.where(even_lon, got_1[...], got_2[...])
    from_west = jnp.where(even_lon, got_2[...], got_1[...])
    ghost = jnp.where(odd, from_west, from_east)
    mine = pairs[...]
    face = faces[...] * jnp.where(odd, turned(from_west, 1), turned(from_east, -1))
    face = jnp.where(lane72 < 32, face, turned(face, 32))
    gain = turned(face * (ghost - mine), 64)
    edge_u[...] = mine + gain
    edge_g[...] = jnp.where(row72 < ROWS, ghost - gain, gain)
    edge_c[...] = face

    lane = lanes(ROWS)
    lane1 = lanes(1)
    row = lax.broadcasted_iota(jnp.int32, (ROWS, COLS), 0)
    first, last = lane == 0, lane == COLS - 1
    side = first | last
    side1 = (lane1 == 0) | (lane1 == COLS - 1)

    def copy(m, l):
        return pltpu.make_async_copy(held.at[m, l], out.at[m, l], sem.at[m, l])

    def line(q, l):
        return rows[pl.ds(q * LEVELS + l, 1), :]

    def level(l, carry):
        k = mask[l].astype(F32)
        e = east[l]
        n = north[l]
        w = jnp.where(first, turned(edge_c[0:ROWS, :], COLS - 1 - 2 * l), turned(e, 1))
        s = jnp.where(row == 0, line(8, l), pltpu.roll(n, 1, 0))
        for m in range(2):
            shift = 63 - m * 32 - 2 * l
            u = u1[m, l]
            u = jnp.where(row == 0, u + line(m, l), u)
            u = jnp.where(row == ROWS - 1, u + line(2 + m, l), u)
            ghosts = turned(edge_g[...], shift)
            u = jnp.where(side, turned(edge_u[0:ROWS, :], shift), u)
            below = line(4 + m, l) + jnp.where(side1, ghosts[ROWS : ROWS + 1, :], 0.0)
            above = line(6 + m, l) + jnp.where(side1, ghosts[ROWS + 1 : ROWS + 2, :], 0.0)
            u_e = jnp.where(last, ghosts[0:ROWS, :], turned(u, -1))
            u_w = jnp.where(first, ghosts[0:ROWS, :], turned(u, 1))
            u_n = jnp.where(row == ROWS - 1, above, pltpu.roll(u, ROWS - 1, 0))
            u_s = jnp.where(row == 0, below, pltpu.roll(u, 1, 0))
            flux = e * (u_e - u) - w * (u - u_w)
            flux = flux + n * (u_n - u) - s * (u - u_s)
            held[m, l] = k * (u + flux)
            copy(m, l).start()
        return carry

    lax.fori_loop(0, LEVELS, level, 0)

    def finish(l, carry):
        for m in range(2):
            copy(m, l).wait()
        return carry

    lax.fori_loop(0, LEVELS, finish, 0)


def block(shape, row):
    lead = len(shape) - 2
    return pl.BlockSpec(shape, lambda i: (0,) * lead + (row, 0))


def struct(*shape):
    return jax.ShapeDtypeStruct(shape, F32)


def cost(us):
    return pl.CostEstimate(flops=int(us * 4e6), bytes_accessed=int(us * 3e6), transcendentals=0)


PARAMS = pltpu.CompilerParams(vmem_limit_bytes=32 * 1024 * 1024)


def local(noise, land_mask, east_coef, north_coef):
    n_lat, n_lon = lax.axis_size("lat"), lax.axis_size("lon")
    member_rows = [block((2, LEVELS, 8, COLS), 0), block((2, LEVELS, 8, COLS), ROWS // 8 - 1)]
    level_rows = [block((LEVELS, 8, COLS), 0), block((LEVELS, 8, COLS), ROWS // 8 - 1)]
    message = struct(6 * LEVELS, COLS)
    send_b, send_a = pl.pallas_call(
        edge_rows,
        grid=(1,),
        in_specs=member_rows + level_rows * 3,
        out_specs=[pl.BlockSpec((6 * LEVELS, COLS), lambda i: (0, 0))] * 2,
        out_shape=[message] * 2,
        compiler_params=PARAMS,
        cost_estimate=cost(1),
        name="edge_rows",
    )(noise, noise, land_mask, land_mask, east_coef, east_coef, north_coef, north_coef)

    route_b = [(i, i ^ 1) for i in range(n_lat)]
    route_a = []
    for k in range(n_lon):
        for i in range(1, n_lat - 1):
            route_a.append((i * n_lon + k, (((i - 1) ^ 1) + 1) * n_lon + k))
        route_a.append(((n_lat - 1) * n_lon + k, n_lat * n_lon - 1 - k))
    got_b = lax.ppermute(send_b, "lat", route_b)
    got_a = lax.ppermute(send_a, ("lat", "lon"), route_a)

    u1, pairs, faces = pl.pallas_call(
        first_step,
        in_specs=[VMEM] * 4,
        out_specs=[VMEM] * 3,
        out_shape=[struct(2, LEVELS, ROWS, COLS), struct(ROWS, COLS), struct(ROWS, COLS)],
        compiler_params=PARAMS,
        cost_estimate=cost(2),
        name="first_step",
    )(noise, land_mask, east_coef, north_coef)

    packed = struct(PACKED, COLS)
    send_1, send_2, pairs, faces, rows = pl.pallas_call(
        join_rows,
        in_specs=[VMEM] * 6,
        out_specs=[VMEM] * 5,
        out_shape=[packed] * 4 + [struct(9 * LEVELS, COLS)],
        scratch_shapes=[pltpu.VMEM((COLS, COLS), F32)] * 3,
        compiler_params=PARAMS,
        cost_estimate=cost(1),
        name="join_rows",
    )(send_b, send_a, got_b, got_a, pairs, faces)

    route_1 = [(k, k ^ 1) for k in range(n_lon)]
    route_2 = [(k, (((k + n_lon - 1) % n_lon ^ 1) + 1) % n_lon) for k in range(n_lon)]
    got_1 = lax.ppermute(send_1, "lon", route_1)
    got_2 = lax.ppermute(send_2, "lon", route_2)

    return pl.pallas_call(
        second_step,
        in_specs=[VMEM] * 9,
        out_specs=pl.BlockSpec(memory_space=pl.ANY),
        out_shape=struct(2, LEVELS, ROWS, COLS),
        scratch_shapes=[pltpu.VMEM((PACKED, COLS), F32)] * 3
        + [pltpu.VMEM((2, LEVELS, ROWS, COLS), F32), pltpu.SemaphoreType.DMA((2, LEVELS))],
        compiler_params=PARAMS,
        cost_estimate=cost(2),
        name="second_step",
    )(u1, land_mask, east_coef, north_coef, got_1, got_2, pairs, faces, rows)


def solution(mesh):
    return jax.shard_map(
        local,
        mesh=mesh,
        in_specs=(
            P(None, None, "lat", "lon"),
            P(None, "lat", "lon"),
            P(None, "lat", "lon"),
            P(None, "lat", "lon"),
        ),
        out_specs=P(None, None, "lat", "lon"),
        check_vma=False,
    )
```

```python
import jax
import jax.numpy as jnp
from jax import lax
from jax.experimental import pallas as pl
from jax.experimental.pallas import tpu as pltpu
from jax.sharding import PartitionSpec as P


LEVELS, ROWS, COLS = 16, 64, 128
PACKED = 72
NORTH, SOUTH = 64, 71
F32 = jnp.float32
VMEM = pl.BlockSpec(memory_space=pltpu.VMEM)
HBM = pl.BlockSpec(memory_space=pltpu.HBM)


def lanes(rows):
    return lax.broadcasted_iota(jnp.int32, (rows, COLS), 1)


def turned(x, shift):
    return pltpu.roll(x, shift % COLS if isinstance(shift, int) else shift, 1)


def slid(x, shift):
    return pltpu.roll(x, shift % x.shape[0], 0)


def edge_rows(noise, mask, east, north, out_b, out_a, noise_at, mask_at, east_at, north_at, sem):
    copies = []
    for k, (whole, part) in enumerate(((noise, noise_at), (mask, mask_at), (east, east_at), (north, north_at))):
        for end in range(2):
            span = pl.ds(end * (ROWS - 2), 2)
            source = whole.at[:, :, span, :] if k == 0 else whole.at[:, span, :]
            copies.append(pltpu.make_async_copy(source, part.at[end], sem.at[k, end]))
    for copy in copies:
        copy.start()
    lat = lax.axis_index("lat")
    top_block = lat == lax.axis_size("lat") - 1
    even = lax.rem(lat, 2) == 0
    lane = lanes(LEVELS)

    def lateral(u, east, west):
        return east * (turned(u, -1) - u) - west * (u - turned(u, 1))

    def inner_faces(east):
        return jnp.where(lane == COLS - 1, 0.0, east), jnp.where(lane == 0, 0.0, turned(east, 1))

    for copy in copies:
        copy.wait()
    mask_t = mask_at[1, :, 1, :].astype(F32)
    mask_t2 = mask_at[1, :, 0, :].astype(F32)
    mask_b = mask_at[0, :, 0, :].astype(F32)
    mask_b2 = mask_at[0, :, 1, :].astype(F32)
    full_t, full_b = east_at[1, :, 1, :], east_at[0, :, 0, :]
    east_t, west_t = inner_faces(full_t)
    east_b, west_b = inner_faces(full_b)
    south_t = north_at[1, :, 0, :]
    north_b = north_at[0, :, 0, :]
    top, bottom = [], []
    top_p, bottom_p = [], []
    for m in range(2):
        u = noise_at[1, m, :, 1, :] * mask_t
        v = noise_at[1, m, :, 0, :] * mask_t2
        top.append(u)
        top_p.append(mask_t * (u + lateral(u, east_t, west_t) - south_t * (u - v)))
        u = noise_at[0, m, :, 0, :] * mask_b
        v = noise_at[0, m, :, 1, :] * mask_b2
        bottom.append(u)
        bottom_p.append(mask_b * (u + lateral(u, east_b, west_b) + north_b * (v - u)))
    top += top_p + [north_at[1, :, 1, :] * mask_t, full_t * mask_t]
    bottom += bottom_p + [mask_b, full_b * mask_b]
    flip = jnp.where(top_block, COLS - 1 - lane, lane)
    for q in range(6):
        rows = pl.ds(q * LEVELS, LEVELS)
        out_b[rows, :] = jnp.where(even, top[q], bottom[q])
        crossed = jnp.take_along_axis(top[q], flip, axis=1)
        out_a[rows, :] = jnp.where(even, bottom[q], crossed)


CHUNK = 4


def first_step(
    noise, mask, east, north, out_u0, out_u1, out_values, out_east, out_north, out_mask, held_east, held_north, held_mask, sem
):
    out_u = (out_u0, out_u1)

    def copies(c):
        span = pl.ds(c * CHUNK, CHUNK)
        pairs = [(noise.at[0, span], out_u0.at[span]), (noise.at[1, span], out_u1.at[span])]
        pairs += [(mask.at[span], held_mask.at[span]), (east.at[span], held_east.at[span])]
        pairs += [(north.at[span], held_north.at[span])]
        return [pltpu.make_async_copy(a, b, sem.at[c, k]) for k, (a, b) in enumerate(pairs)]

    for c in range(LEVELS // CHUNK):
        for copy in copies(c):
            copy.start()
    lane = lanes(ROWS)
    row = lax.broadcasted_iota(jnp.int32, (ROWS, COLS), 0)
    group = lane // 4

    def level(l, carry):
        values, easts, norths, masks = carry
        k = held_mask[l].astype(F32)
        e_all = held_east[l]
        n_all = held_north[l]
        e = jnp.where(lane == COLS - 1, 0.0, e_all)
        w = jnp.where(lane == 0, 0.0, turned(e_all, 1))
        n = jnp.where(row == ROWS - 1, 0.0, n_all)
        s = jnp.where(row == 0, 0.0, slid(n_all, 1))
        here = group == l
        shift = 4 * l + 2
        easts = jnp.where(here, turned(e_all * k, shift), easts)
        norths = jnp.where(here, turned(n_all, shift), norths)
        masks = jnp.where(here, turned(k, shift), masks)
        for m in range(2):
            u = out_u[m][l] * k
            u_e, u_w = turned(u, -1), turned(u, 1)
            flux = e * (u_e - u) - w * (u - u_w)
            flux = flux + n * (slid(u, -1) - u) - s * (u - slid(u, 1))
            v = k * (u + flux)
            out_u[m][l] = v
            edges = jnp.where(lane == COLS - 2, u_e, jnp.where(lane == 1, u_w, v))
            values = jnp.where(group == m * 16 + l, turned(edges, 64 * m + shift), values)
        return values, easts, norths, masks

    carry = (jnp.zeros((ROWS, COLS), F32),) * 4
    for c in range(LEVELS // CHUNK):
        for copy in copies(c):
            copy.wait()
        carry = lax.fori_loop(c * CHUNK, (c + 1) * CHUNK, level, carry)
    values, easts, norths, masks = carry
    out_values[...] = values
    for out, x in ((out_east, easts), (out_north, norths), (out_mask, masks)):
        out[...] = jnp.where(lane < 64, x, turned(x, 64))


def join_rows(
    own_b, own_a, got_b, got_a, values, easts, norths, masks,
    send_1, send_2, out_values, out_east, out_north, out_mask, out_rows, south, north, side
):
    lat = lax.axis_index("lat")
    top_block = lat == lax.axis_size("lat") - 1
    even = lax.rem(lat, 2) == 0
    even_lon = lax.rem(lax.axis_index("lon"), 2) == 0

    def part(q):
        rows = pl.ds(q * LEVELS, LEVELS)
        ob, oa, gb, ga = own_b[rows, :], own_a[rows, :], got_b[rows, :], got_a[rows, :]
        return ob, oa, jnp.where(even, gb, ga), jnp.where(even, ga, gb)

    flip = COLS - 1 - lanes(LEVELS)

    def own(q):
        ob, oa, _, _ = part(q)
        back = jnp.where(top_block, jnp.take_along_axis(oa, flip, axis=1), oa)
        return jnp.where(even, ob, back), jnp.where(even, oa, ob)

    def put(ref, half, slots, x):
        for j in slots:
            ref[pl.ds(half * 64 + j, LEVELS, stride=4), :] = x

    own_n, own_k = own(4)
    _, _, far_n, far_s = part(4)
    ghost_n = jnp.where(top_block, far_n, own_n * far_n)
    for m in range(2):
        own_t, own_bot = own(m)
        _, _, up, down = part(m)
        _, _, up_p, down_p = part(2 + m)
        gain_s = own_k * far_s * (down - own_bot)
        gain_n = own_n * (up - own_t)
        out_rows[pl.ds(m * LEVELS, LEVELS), :] = gain_s
        out_rows[pl.ds((2 + m) * LEVELS, LEVELS), :] = gain_n
        out_rows[pl.ds((4 + m) * LEVELS, LEVELS), :] = down_p - far_s * (down - own_bot)
        out_rows[pl.ds((6 + m) * LEVELS, LEVELS), :] = up_p - ghost_n * (up - own_t)
        put(south, m, (0, 3), down)
        put(south, m, (1, 2), gain_s)
        put(north, m, (0, 3), up)
        put(north, m, (1, 2), gain_n)
    out_rows[pl.ds(8 * LEVELS, LEVELS), :] = far_s
    _, _, up_e, down_e = part(5)
    put(side, 0, (0, 1), down_e)
    put(side, 0, (2, 3), far_s)
    put(side, 1, (0, 1, 2, 3), up_e)

    lane1 = lanes(1)
    slot1 = lax.rem(lane1, 4)
    turned_s = jnp.transpose(south[...])
    turned_n = jnp.transpose(north[...])
    turned_c = jnp.transpose(side[...])
    row_s = jnp.where(slot1 >= 2, turned_s[0:1, :], turned_s[COLS - 1 : COLS, :])
    row_n = jnp.where(slot1 >= 2, turned_n[0:1, :], turned_n[COLS - 1 : COLS, :])
    inner = (slot1 == 1) | (slot1 == 2)
    low_half = lane1 < 64
    first_c, last_c = turned_c[0:1, :], turned_c[COLS - 1 : COLS, :]
    face_s = jnp.where(low_half, last_c, turned(last_c, 64))
    coef_s = jnp.where(slot1 == 1, turned(last_c, -1), first_c)
    coef_s = jnp.where(low_half, coef_s, turned(coef_s, 64))
    face_n = jnp.where(low_half, turned(last_c, 64), last_c)
    mirrored = jnp.where(low_half, turned(first_c, 64), first_c)

    def extend(out, x, north_row, south_row):
        out[0:ROWS, :] = x[...]
        out[ROWS:PACKED, :] = jnp.zeros((PACKED - ROWS, COLS), F32)
        out[NORTH : NORTH + 1, :] = north_row
        out[SOUTH : SOUTH + 1, :] = south_row

    one = jnp.ones((1, COLS), F32)
    extend(out_values, values, row_n, row_s)
    out_values[0:1, :] = values[0:1, :] + jnp.where(inner, row_s, 0.0)
    out_values[ROWS - 1 : ROWS, :] = values[ROWS - 1 : ROWS, :] + jnp.where(inner, row_n, 0.0)
    extend(out_east, easts, jnp.where(top_block, one, face_n), face_s)
    extend(out_mask, masks, jnp.where(top_block, mirrored, one), one)
    extend(out_north, norths, jnp.zeros((1, COLS), F32), coef_s)
    slot = lax.rem(lanes(PACKED), 4)
    x = out_values[...]
    eastward = jnp.where(slot >= 2, turned(x, 2), out_east[...])
    westward = jnp.where(slot < 2, turned(x, -2), out_mask[...])
    send_1[...] = jnp.where(even_lon, eastward, westward)
    send_2[...] = jnp.where(even_lon, westward, eastward)


def second_step(u1_0, u1_1, mask, east, north, rows, out):
    u1 = (u1_0, u1_1)
    lane = lanes(ROWS)
    row = lax.broadcasted_iota(jnp.int32, (ROWS, COLS), 0)

    def line(q, l):
        return rows[pl.ds(q * LEVELS + l, 1), :]

    def level(l, carry):
        k = mask[l].astype(F32)
        e_all = east[l]
        n = north[l]
        e = jnp.where(lane == COLS - 1, 0.0, e_all)
        w = jnp.where(lane == 0, 0.0, turned(e_all, 1))
        s = jnp.where(row == 0, line(8, l), slid(n, 1))
        for m in range(2):
            u = u1[m][l]
            u = jnp.where(row == 0, u + line(m, l), u)
            u = jnp.where(row == ROWS - 1, u + line(2 + m, l), u)
            u_n = jnp.where(row == ROWS - 1, line(6 + m, l), slid(u, -1))
            u_s = jnp.where(row == 0, line(4 + m, l), slid(u, 1))
            flux = e * (turned(u, -1) - u) - w * (u - turned(u, 1))
            flux = flux + n * (u_n - u) - s * (u - u_s)
            out[m, l] = k * (u + flux)
        return carry

    lax.fori_loop(0, LEVELS, level, 0)


def join_columns(u2, got_1, got_2, values, easts, norths, masks, out, gain, held, sem):
    even_lon = lax.rem(lax.axis_index("lon"), 2) == 0
    slot = lax.rem(lanes(PACKED), 4)
    is_east = slot == 1
    inner = is_east | (slot == 2)
    from_east = jnp.where(even_lon, got_1[...], got_2[...])
    from_west = jnp.where(even_lon, got_2[...], got_1[...])
    x, e, n, k = values[...], easts[...], norths[...], masks[...]
    own_0 = jnp.where(is_east, turned(x, 1), turned(x, -1))
    ghost_0 = jnp.where(is_east, from_east, from_west)
    ghost_1 = jnp.where(is_east, turned(from_east, 1), turned(from_west, -1))
    face = jnp.where(is_east, e * turned(from_east, -1), k * turned(from_west, 1))
    d = jnp.where(inner, face * (ghost_0 - own_0), 0.0)
    inside = jnp.where(is_east, turned(e, 1), e)
    s = slid(n, 1)
    change = d * (1.0 - inside - n - s) + face * (ghost_1 - x - d - d) + n * slid(d, -1) + s * slid(d, 1)
    beside = inside * d
    beside = jnp.where(slot == 0, turned(beside, -1), turned(beside, 1))
    gain[...] = k * jnp.where(inner, change, beside)

    lane = lanes(ROWS)
    edge = (lane < 2) | (lane >= COLS - 2)

    def copy(m, c):
        span = pl.ds(c * CHUNK, CHUNK)
        return pltpu.make_async_copy(held.at[m, span], out.at[m, span], sem.at[m, c])

    for c in range(LEVELS // CHUNK):
        for m in range(2):
            for l in range(c * CHUNK, (c + 1) * CHUNK):
                change = turned(gain[0:ROWS, :], 126 - 64 * m - 4 * l)
                held[m, l] = u2[m, l] + jnp.where(edge, change, 0.0)
            copy(m, c).start()
    for c in range(LEVELS // CHUNK):
        for m in range(2):
            copy(m, c).wait()


def struct(*shape):
    return jax.ShapeDtypeStruct(shape, F32)


def kernel(body, name, inputs, outputs, us, scratch=(), space=VMEM, limit=16):
    return pl.pallas_call(
        body,
        in_specs=[space] * inputs,
        out_specs=[VMEM if body is not join_columns else HBM] * len(outputs),
        out_shape=outputs,
        scratch_shapes=list(scratch),
        compiler_params=pltpu.CompilerParams(vmem_limit_bytes=limit * 1024 * 1024),
        cost_estimate=pl.CostEstimate(flops=int(us * 4e6), bytes_accessed=int(us * 3e6), transcendentals=0),
        name=name,
    )


def local(noise, land_mask, east_coef, north_coef):
    n_lat, n_lon = lax.axis_size("lat"), lax.axis_size("lon")
    message = struct(6 * LEVELS, COLS)
    ends = pltpu.VMEM((2, LEVELS, 2, COLS), F32)
    scratch = [
        pltpu.VMEM((2, 2, LEVELS, 2, COLS), F32),
        pltpu.VMEM((2, LEVELS, 2, COLS), jnp.int32),
        ends,
        ends,
        pltpu.SemaphoreType.DMA((4, 2)),
    ]
    send_b, send_a = kernel(edge_rows, "edge_rows", 4, [message] * 2, 1, scratch, HBM, 63)(
        noise, land_mask, east_coef, north_coef
    )

    route_b = [(i, i ^ 1) for i in range(n_lat)]
    route_a = []
    for k in range(n_lon):
        for i in range(1, n_lat - 1):
            route_a.append((i * n_lon + k, (((i - 1) ^ 1) + 1) * n_lon + k))
        route_a.append(((n_lat - 1) * n_lon + k, n_lat * n_lon - 1 - k))
    got_a = lax.ppermute(send_a, ("lat", "lon"), route_a)
    got_b = lax.ppermute(send_b, "lat", route_b)

    whole, plane, packed = struct(2, LEVELS, ROWS, COLS), struct(ROWS, COLS), struct(PACKED, COLS)
    coef, levels = struct(LEVELS, ROWS, COLS), jax.ShapeDtypeStruct((LEVELS, ROWS, COLS), jnp.int32)
    outs = [coef] * 2 + [plane] * 4 + [coef] * 2 + [levels]
    scratch = [pltpu.SemaphoreType.DMA((LEVELS // CHUNK, 5))]
    u1_0, u1_1, *columns, east, north, mask = kernel(first_step, "first_step", 4, outs, 2, scratch, HBM, 51)(
        noise, land_mask, east_coef, north_coef
    )
    square = pltpu.VMEM((COLS, COLS), F32)
    send_1, send_2, *columns, rows = kernel(
        join_rows, "join_rows", 8, [packed] * 6 + [struct(9 * LEVELS, COLS)], 1, [square] * 3
    )(send_b, send_a, got_b, got_a, *columns)

    route_1 = [(k, k ^ 1) for k in range(n_lon)]
    route_2 = [(k, (((k + n_lon - 1) % n_lon ^ 1) + 1) % n_lon) for k in range(n_lon)]
    got_2 = lax.ppermute(send_2, "lon", route_2)
    got_1 = lax.ppermute(send_1, "lon", route_1)

    (u2,) = kernel(second_step, "second_step", 6, [whole], 2)(u1_0, u1_1, mask, east, north, rows)
    scratch = [pltpu.VMEM((PACKED, COLS), F32), pltpu.VMEM(whole.shape, F32), pltpu.SemaphoreType.DMA((2, LEVELS // CHUNK))]
    return kernel(join_columns, "join_columns", 7, [whole], 1, scratch)(u2, got_1, got_2, *columns)[0]


def solution(mesh):
    return jax.shard_map(
        local,
        mesh=mesh,
        in_specs=(
            P(None, None, "lat", "lon"),
            P(None, "lat", "lon"),
            P(None, "lat", "lon"),
            P(None, "lat", "lon"),
        ),
        out_specs=P(None, None, "lat", "lon"),
        check_vma=False,
    )
```

```python
import jax
import jax.numpy as jnp
from jax import lax
from jax.experimental import pallas as pl
from jax.experimental.pallas import tpu as pltpu
from jax.sharding import PartitionSpec as P


LEVELS, ROWS, COLS = 16, 64, 128
PACKED = 72
NORTH, SOUTH = 64, 71
F32 = jnp.float32
VMEM = pl.BlockSpec(memory_space=pltpu.VMEM)
HBM = pl.BlockSpec(memory_space=pltpu.HBM)


def lanes(rows):
    return lax.broadcasted_iota(jnp.int32, (rows, COLS), 1)


def turned(x, shift):
    return pltpu.roll(x, shift % COLS if isinstance(shift, int) else shift, 1)


def slid(x, shift):
    return pltpu.roll(x, shift % x.shape[0], 0)


def edge_rows(noise, mask, east, north, out_a, out_b, noise_at, mask_at, east_at, north_at, sem):
    copies = []
    for k, (whole, part) in enumerate(((noise, noise_at), (mask, mask_at), (east, east_at), (north, north_at))):
        for end in range(2):
            span = pl.ds(end * (ROWS - 2), 2)
            source = whole.at[:, :, span, :] if k == 0 else whole.at[:, span, :]
            copies.append(pltpu.make_async_copy(source, part.at[end], sem.at[k, end]))
    for copy in copies:
        copy.start()
    lat = lax.axis_index("lat")
    top_block = lat == lax.axis_size("lat") - 1
    even = lax.rem(lat, 2) == 0
    lane = lanes(LEVELS)

    def lateral(u, east, west):
        return east * (turned(u, -1) - u) - west * (u - turned(u, 1))

    def inner_faces(east):
        return jnp.where(lane == COLS - 1, 0.0, east), jnp.where(lane == 0, 0.0, turned(east, 1))

    for copy in copies:
        copy.wait()
    mask_t = mask_at[1, :, 1, :].astype(F32)
    mask_t2 = mask_at[1, :, 0, :].astype(F32)
    mask_b = mask_at[0, :, 0, :].astype(F32)
    mask_b2 = mask_at[0, :, 1, :].astype(F32)
    full_t, full_b = east_at[1, :, 1, :], east_at[0, :, 0, :]
    east_t, west_t = inner_faces(full_t)
    east_b, west_b = inner_faces(full_b)
    south_t = north_at[1, :, 0, :]
    north_b = north_at[0, :, 0, :]
    top, bottom = [], []
    top_p, bottom_p = [], []
    for m in range(2):
        u = noise_at[1, m, :, 1, :] * mask_t
        v = noise_at[1, m, :, 0, :] * mask_t2
        top.append(u)
        top_p.append(mask_t * (u + lateral(u, east_t, west_t) - south_t * (u - v)))
        u = noise_at[0, m, :, 0, :] * mask_b
        v = noise_at[0, m, :, 1, :] * mask_b2
        bottom.append(u)
        bottom_p.append(mask_b * (u + lateral(u, east_b, west_b) + north_b * (v - u)))
    top += top_p + [north_at[1, :, 1, :] * mask_t, full_t * mask_t]
    bottom += bottom_p + [mask_b, full_b * mask_b]
    flip = jnp.where(top_block, COLS - 1 - lane, lane)
    for q in range(6):
        rows = pl.ds(q * LEVELS, LEVELS)
        out_b[rows, :] = jnp.where(even, top[q], bottom[q])
        crossed = jnp.take_along_axis(top[q], flip, axis=1)
        out_a[rows, :] = jnp.where(even, bottom[q], crossed)


CHUNK = 4
FETCH = 4


def first_step(
    noise, mask, east, north, out_u0, out_u1, out_values, out_east, out_north, out_mask, held_east, held_north, held_mask, edges, sem
):
    out_u = (out_u0, out_u1)

    def copies(c):
        span = pl.ds(c * FETCH, FETCH)
        pairs = [(noise.at[0, span], out_u0.at[span]), (noise.at[1, span], out_u1.at[span])]
        pairs += [(mask.at[span], held_mask.at[span]), (east.at[span], held_east.at[span])]
        pairs += [(north.at[span], held_north.at[span])]
        return [pltpu.make_async_copy(a, b, sem.at[c, k]) for k, (a, b) in enumerate(pairs)]

    for c in range(min(LEVELS // FETCH, 99)):
        for copy in copies(c):
            copy.start()
    lane = lanes(ROWS)
    row = lax.broadcasted_iota(jnp.int32, (ROWS, COLS), 0)
    group = lane // 4

    def place(out, x, at):
        pltpu.store(out, turned(x, 4 * at + 2), mask=group == at)

    def level(l):
        k = held_mask[l].astype(F32)
        e_all = held_east[l]
        n_all = held_north[l]
        e = jnp.where(lane == COLS - 1, 0.0, e_all)
        w = jnp.where(lane == 0, 0.0, turned(e_all, 1))
        n = jnp.where(row == ROWS - 1, 0.0, n_all)
        s = jnp.where(row == 0, 0.0, slid(n_all, 1))
        for m in range(2):
            u = out_u[m][l] * k
            u_e, u_w = turned(u, -1), turned(u, 1)
            flux = e * (u_e - u) - w * (u - u_w)
            flux = flux + n * (slid(u, -1) - u) - s * (u - slid(u, 1))
            v = k * (u + flux)
            out_u[m][l] = v
            edges[m * LEVELS + l] = jnp.where(lane == COLS - 2, u_e, jnp.where(lane == 1, u_w, v))

    for c in range(LEVELS // FETCH):
        for copy in copies(c):
            copy.wait()
        for l in range(c * FETCH, (c + 1) * FETCH):
            level(l)
    for l in range(LEVELS):
        k = held_mask[l].astype(F32)
        place(out_east, held_east[l] * k, l)
        place(out_north, held_north[l], l)
        place(out_mask, k, l)
        for m in range(2):
            place(out_values, edges[m * LEVELS + l], m * LEVELS + l)
    for out in (out_east, out_north, out_mask):
        out[...] = jnp.where(lane < 64, out[...], turned(out[...], 64))


def join_rows(
    own_a, own_b, got_a, got_b, values, easts, norths, masks,
    send_2, send_1, out_values, out_east, out_north, out_mask, out_rows, south, north, side
):
    lat = lax.axis_index("lat")
    top_block = lat == lax.axis_size("lat") - 1
    even = lax.rem(lat, 2) == 0
    even_lon = lax.rem(lax.axis_index("lon"), 2) == 0

    def part(q):
        rows = pl.ds(q * LEVELS, LEVELS)
        ob, oa, gb, ga = own_b[rows, :], own_a[rows, :], got_b[rows, :], got_a[rows, :]
        return ob, oa, jnp.where(even, gb, ga), jnp.where(even, ga, gb)

    flip = COLS - 1 - lanes(LEVELS)

    def own(q):
        ob, oa, _, _ = part(q)
        back = jnp.where(top_block, jnp.take_along_axis(oa, flip, axis=1), oa)
        return jnp.where(even, ob, back), jnp.where(even, oa, ob)

    def put(ref, half, slots, x):
        for j in slots:
            ref[pl.ds(half * 64 + j, LEVELS, stride=4), :] = x

    own_n, own_k = own(4)
    _, _, far_n, far_s = part(4)
    ghost_n = jnp.where(top_block, far_n, own_n * far_n)
    for m in range(2):
        own_t, own_bot = own(m)
        _, _, up, down = part(m)
        _, _, up_p, down_p = part(2 + m)
        gain_s = own_k * far_s * (down - own_bot)
        gain_n = own_n * (up - own_t)
        out_rows[pl.ds(m * LEVELS, LEVELS), :] = gain_s
        out_rows[pl.ds((2 + m) * LEVELS, LEVELS), :] = gain_n
        out_rows[pl.ds((4 + m) * LEVELS, LEVELS), :] = down_p - far_s * (down - own_bot)
        out_rows[pl.ds((6 + m) * LEVELS, LEVELS), :] = up_p - ghost_n * (up - own_t)
        put(south, m, (0, 3), down)
        put(south, m, (1, 2), gain_s)
        put(north, m, (0, 3), up)
        put(north, m, (1, 2), gain_n)
    out_rows[pl.ds(8 * LEVELS, LEVELS), :] = far_s
    _, _, up_e, down_e = part(5)
    put(side, 0, (0, 1), down_e)
    put(side, 0, (2, 3), far_s)
    put(side, 1, (0, 1, 2, 3), up_e)

    lane1 = lanes(1)
    slot1 = lax.rem(lane1, 4)
    turned_s = jnp.transpose(south[...])
    turned_n = jnp.transpose(north[...])
    turned_c = jnp.transpose(side[...])
    row_s = jnp.where(slot1 >= 2, turned_s[0:1, :], turned_s[COLS - 1 : COLS, :])
    row_n = jnp.where(slot1 >= 2, turned_n[0:1, :], turned_n[COLS - 1 : COLS, :])
    inner = (slot1 == 1) | (slot1 == 2)
    low_half = lane1 < 64
    first_c, last_c = turned_c[0:1, :], turned_c[COLS - 1 : COLS, :]
    face_s = jnp.where(low_half, last_c, turned(last_c, 64))
    coef_s = jnp.where(slot1 == 1, turned(last_c, -1), first_c)
    coef_s = jnp.where(low_half, coef_s, turned(coef_s, 64))
    face_n = jnp.where(low_half, turned(last_c, 64), last_c)
    mirrored = jnp.where(low_half, turned(first_c, 64), first_c)

    def extend(out, x, north_row, south_row):
        out[0:ROWS, :] = x[...]
        out[ROWS:PACKED, :] = jnp.zeros((PACKED - ROWS, COLS), F32)
        out[NORTH : NORTH + 1, :] = north_row
        out[SOUTH : SOUTH + 1, :] = south_row

    one = jnp.ones((1, COLS), F32)
    extend(out_values, values, row_n, row_s)
    out_values[0:1, :] = values[0:1, :] + jnp.where(inner, row_s, 0.0)
    out_values[ROWS - 1 : ROWS, :] = values[ROWS - 1 : ROWS, :] + jnp.where(inner, row_n, 0.0)
    extend(out_east, easts, jnp.where(top_block, one, face_n), face_s)
    extend(out_mask, masks, jnp.where(top_block, mirrored, one), one)
    extend(out_north, norths, jnp.zeros((1, COLS), F32), coef_s)
    slot = lax.rem(lanes(PACKED), 4)
    x = out_values[...]
    eastward = jnp.where(slot >= 2, turned(x, 2), out_east[...])
    westward = jnp.where(slot < 2, turned(x, -2), out_mask[...])
    send_1[...] = jnp.where(even_lon, eastward, westward)
    send_2[...] = jnp.where(even_lon, westward, eastward)


def second_step(u1_0, u1_1, mask, east, north, rows, out):
    u1 = (u1_0, u1_1)
    lane = lanes(ROWS)
    row = lax.broadcasted_iota(jnp.int32, (ROWS, COLS), 0)

    def line(q, l):
        return rows[pl.ds(q * LEVELS + l, 1), :]

    def level(l):
        k = mask[l].astype(F32)
        e_all = east[l]
        n = north[l]
        e = jnp.where(lane == COLS - 1, 0.0, e_all)
        w = jnp.where(lane == 0, 0.0, turned(e_all, 1))
        s = jnp.where(row == 0, line(8, l), slid(n, 1))
        for m in range(2):
            u = u1[m][l]
            u = jnp.where(row == 0, u + line(m, l), u)
            u = jnp.where(row == ROWS - 1, u + line(2 + m, l), u)
            u_n = jnp.where(row == ROWS - 1, line(6 + m, l), slid(u, -1))
            u_s = jnp.where(row == 0, line(4 + m, l), slid(u, 1))
            flux = e * (turned(u, -1) - u) - w * (u - turned(u, 1))
            flux = flux + n * (u_n - u) - s * (u - u_s)
            out[m, l] = k * (u + flux)

    for l in range(LEVELS):
        level(l)


def join_columns(u2, got_2, got_1, values, easts, norths, masks, out, gain, held, sem):
    even_lon = lax.rem(lax.axis_index("lon"), 2) == 0
    slot = lax.rem(lanes(PACKED), 4)
    is_east = slot == 1
    inner = is_east | (slot == 2)
    from_east = jnp.where(even_lon, got_1[...], got_2[...])
    from_west = jnp.where(even_lon, got_2[...], got_1[...])
    x, e, n, k = values[...], easts[...], norths[...], masks[...]
    own_0 = jnp.where(is_east, turned(x, 1), turned(x, -1))
    ghost_0 = jnp.where(is_east, from_east, from_west)
    ghost_1 = jnp.where(is_east, turned(from_east, 1), turned(from_west, -1))
    face = jnp.where(is_east, e * turned(from_east, -1), k * turned(from_west, 1))
    d = jnp.where(inner, face * (ghost_0 - own_0), 0.0)
    inside = jnp.where(is_east, turned(e, 1), e)
    s = slid(n, 1)
    change = d * (1.0 - inside - n - s) + face * (ghost_1 - x - d - d) + n * slid(d, -1) + s * slid(d, 1)
    beside = inside * d
    beside = jnp.where(slot == 0, turned(beside, -1), turned(beside, 1))
    gain[...] = k * jnp.where(inner, change, beside)

    lane = lanes(ROWS)
    edge = (lane < 2) | (lane >= COLS - 2)

    def copy(m, c):
        span = pl.ds(c * CHUNK, CHUNK)
        return pltpu.make_async_copy(held.at[m, span], out.at[m, span], sem.at[m, c])

    for c in range(LEVELS // CHUNK):
        for m in range(2):
            for l in range(c * CHUNK, (c + 1) * CHUNK):
                change = turned(gain[0:ROWS, :], 126 - 64 * m - 4 * l)
                held[m, l] = u2[m, l] + jnp.where(edge, change, 0.0)
            copy(m, c).start()
    for c in range(LEVELS // CHUNK):
        for m in range(2):
            copy(m, c).wait()


def struct(*shape):
    return jax.ShapeDtypeStruct(shape, F32)


def kernel(body, name, inputs, outputs, us, scratch=(), space=VMEM, limit=16):
    return pl.pallas_call(
        body,
        in_specs=[space] * inputs,
        out_specs=[VMEM if body is not join_columns else HBM] * len(outputs),
        out_shape=outputs,
        scratch_shapes=list(scratch),
        compiler_params=pltpu.CompilerParams(vmem_limit_bytes=limit * 1024 * 1024),
        cost_estimate=pl.CostEstimate(flops=int(us * 4e6), bytes_accessed=int(us * 3e6), transcendentals=0),
        name=name,
    )


def local(noise, land_mask, east_coef, north_coef):
    n_lat, n_lon = lax.axis_size("lat"), lax.axis_size("lon")
    message = struct(6 * LEVELS, COLS)
    ends = pltpu.VMEM((2, LEVELS, 2, COLS), F32)
    scratch = [
        pltpu.VMEM((2, 2, LEVELS, 2, COLS), F32),
        pltpu.VMEM((2, LEVELS, 2, COLS), jnp.int32),
        ends,
        ends,
        pltpu.SemaphoreType.DMA((4, 2)),
    ]
    send_a, send_b = kernel(edge_rows, "edge_rows", 4, [message] * 2, 1, scratch, HBM, 63)(
        noise, land_mask, east_coef, north_coef
    )

    route_b = [(i, i ^ 1) for i in range(n_lat)]
    route_a = []
    for k in range(n_lon):
        for i in range(1, n_lat - 1):
            route_a.append((i * n_lon + k, (((i - 1) ^ 1) + 1) * n_lon + k))
        route_a.append(((n_lat - 1) * n_lon + k, n_lat * n_lon - 1 - k))
    got_a = lax.ppermute(send_a, ("lat", "lon"), route_a)
    got_b = lax.ppermute(send_b, "lat", route_b)

    whole, plane, packed = struct(2, LEVELS, ROWS, COLS), struct(ROWS, COLS), struct(PACKED, COLS)
    coef, levels = struct(LEVELS, ROWS, COLS), jax.ShapeDtypeStruct((LEVELS, ROWS, COLS), jnp.int32)
    outs = [coef] * 2 + [plane] * 4 + [coef] * 2 + [levels]
    scratch = [pltpu.VMEM((2 * LEVELS, ROWS, COLS), F32), pltpu.SemaphoreType.DMA((LEVELS // FETCH, 5))]
    u1_0, u1_1, *columns, east, north, mask = kernel(first_step, "first_step", 4, outs, 2, scratch, HBM, 51)(
        noise, land_mask, east_coef, north_coef
    )
    square = pltpu.VMEM((COLS, COLS), F32)
    send_2, send_1, *columns, rows = kernel(
        join_rows, "join_rows", 8, [packed] * 6 + [struct(9 * LEVELS, COLS)], 1, [square] * 3
    )(send_a, send_b, got_a, got_b, *columns)

    route_1 = [(k, k ^ 1) for k in range(n_lon)]
    route_2 = [(k, (((k + n_lon - 1) % n_lon ^ 1) + 1) % n_lon) for k in range(n_lon)]
    got_2 = lax.ppermute(send_2, "lon", route_2)
    got_1 = lax.ppermute(send_1, "lon", route_1)

    (u2,) = kernel(second_step, "second_step", 6, [whole], 2)(u1_0, u1_1, mask, east, north, rows)
    scratch = [pltpu.VMEM((PACKED, COLS), F32), pltpu.VMEM(whole.shape, F32), pltpu.SemaphoreType.DMA((2, LEVELS // CHUNK))]
    return kernel(join_columns, "join_columns", 7, [whole], 1, scratch)(u2, got_2, got_1, *columns)[0]


def solution(mesh):
    return jax.shard_map(
        local,
        mesh=mesh,
        in_specs=(
            P(None, None, "lat", "lon"),
            P(None, "lat", "lon"),
            P(None, "lat", "lon"),
            P(None, "lat", "lon"),
        ),
        out_specs=P(None, None, "lat", "lon"),
        check_vma=False,
    )
```

```python
import jax
import jax.numpy as jnp
from jax import lax
from jax.experimental import pallas as pl
from jax.experimental.pallas import tpu as pltpu
from jax.sharding import PartitionSpec as P


LEVELS, ROWS, COLS = 16, 64, 128
PACKED = 72
NORTH, SOUTH = 64, 71
F32 = jnp.float32
VMEM = pl.BlockSpec(memory_space=pltpu.VMEM)
HBM = pl.BlockSpec(memory_space=pltpu.HBM)


def lanes(rows):
    return lax.broadcasted_iota(jnp.int32, (rows, COLS), 1)


def turned(x, shift):
    return pltpu.roll(x, shift % COLS if isinstance(shift, int) else shift, 1)


def slid(x, shift):
    return pltpu.roll(x, shift % x.shape[0], 0)


def edge_rows(noise, mask, east, north, out_a, out_b, noise_at, mask_at, east_at, north_at, sem):
    copies = []
    for k, (whole, part) in enumerate(((noise, noise_at), (mask, mask_at), (east, east_at), (north, north_at))):
        for end in range(2):
            span = pl.ds(end * (ROWS - 2), 2)
            source = whole.at[:, :, span, :] if k == 0 else whole.at[:, span, :]
            copies.append(pltpu.make_async_copy(source, part.at[end], sem.at[k, end]))
    for copy in copies:
        copy.start()
    lat = lax.axis_index("lat")
    top_block = lat == lax.axis_size("lat") - 1
    even = lax.rem(lat, 2) == 0
    lane = lanes(LEVELS)

    def lateral(u, east, west):
        return east * (turned(u, -1) - u) - west * (u - turned(u, 1))

    def inner_faces(east):
        return jnp.where(lane == COLS - 1, 0.0, east), jnp.where(lane == 0, 0.0, turned(east, 1))

    for copy in copies:
        copy.wait()
    mask_t = mask_at[1, :, 1, :].astype(F32)
    mask_t2 = mask_at[1, :, 0, :].astype(F32)
    mask_b = mask_at[0, :, 0, :].astype(F32)
    mask_b2 = mask_at[0, :, 1, :].astype(F32)
    full_t, full_b = east_at[1, :, 1, :], east_at[0, :, 0, :]
    east_t, west_t = inner_faces(full_t)
    east_b, west_b = inner_faces(full_b)
    south_t = north_at[1, :, 0, :]
    north_b = north_at[0, :, 0, :]
    top, bottom = [], []
    top_p, bottom_p = [], []
    for m in range(2):
        u = noise_at[1, m, :, 1, :] * mask_t
        v = noise_at[1, m, :, 0, :] * mask_t2
        top.append(u)
        top_p.append(mask_t * (u + lateral(u, east_t, west_t) - south_t * (u - v)))
        u = noise_at[0, m, :, 0, :] * mask_b
        v = noise_at[0, m, :, 1, :] * mask_b2
        bottom.append(u)
        bottom_p.append(mask_b * (u + lateral(u, east_b, west_b) + north_b * (v - u)))
    top += top_p + [north_at[1, :, 1, :] * mask_t, full_t * mask_t]
    bottom += bottom_p + [mask_b, full_b * mask_b]
    flip = jnp.where(top_block, COLS - 1 - lane, lane)
    for q in range(6):
        rows = pl.ds(q * LEVELS, LEVELS)
        out_b[rows, :] = jnp.where(even, top[q], bottom[q])
        crossed = jnp.take_along_axis(top[q], flip, axis=1)
        out_a[rows, :] = jnp.where(even, bottom[q], crossed)


CHUNK = 4
FETCH = 8


def first_step(
    noise, mask, east, north, out_u0, out_u1, out_values, out_east, out_north, out_mask, held_east, held_north, held_mask, edges, sem
):
    out_u = (out_u0, out_u1)

    def copies(c, which):
        span = pl.ds(c * FETCH, FETCH)
        pairs = [(noise.at[0, span], out_u0.at[span]), (noise.at[1, span], out_u1.at[span])]
        pairs += [(mask.at[span], held_mask.at[span]), (east.at[span], held_east.at[span])]
        pairs += [(north.at[span], held_north.at[span])]
        return [pltpu.make_async_copy(*pairs[k], sem.at[c, k]) for k in which]

    fields, coefs = range(2), range(2, 5)
    for which in (coefs, fields):
        for c in range(LEVELS // FETCH):
            for copy in copies(c, which):
                copy.start()
    lane = lanes(ROWS)
    row = lax.broadcasted_iota(jnp.int32, (ROWS, COLS), 0)
    group = lane // 4

    def place(out, x, at):
        pltpu.store(out, turned(x, 4 * at + 2), mask=group == at)

    def level(l):
        k = held_mask[l].astype(F32)
        e_all = held_east[l]
        n_all = held_north[l]
        e = jnp.where(lane == COLS - 1, 0.0, e_all)
        w = jnp.where(lane == 0, 0.0, turned(e_all, 1))
        n = jnp.where(row == ROWS - 1, 0.0, n_all)
        s = jnp.where(row == 0, 0.0, slid(n_all, 1))
        for m in range(2):
            u = out_u[m][l] * k
            u_e, u_w = turned(u, -1), turned(u, 1)
            flux = e * (u_e - u) - w * (u - u_w)
            flux = flux + n * (slid(u, -1) - u) - s * (u - slid(u, 1))
            v = k * (u + flux)
            out_u[m][l] = v
            edges[m * LEVELS + l] = jnp.where(lane == COLS - 2, u_e, jnp.where(lane == 1, u_w, v))

    for c in range(LEVELS // FETCH):
        for copy in copies(c, coefs):
            copy.wait()
        for l in range(c * FETCH, (c + 1) * FETCH):
            k = held_mask[l].astype(F32)
            place(out_east, held_east[l] * k, l)
            place(out_north, held_north[l], l)
            place(out_mask, k, l)
    for c in range(LEVELS // FETCH):
        for copy in copies(c, fields):
            copy.wait()
        for l in range(c * FETCH, (c + 1) * FETCH):
            level(l)
    for g in range(2 * LEVELS):
        place(out_values, edges[g], g)
    for out in (out_east, out_north, out_mask):
        out[...] = jnp.where(lane < 64, out[...], turned(out[...], 64))


def join_rows(
    own_a, own_b, got_a, got_b, values, easts, norths, masks,
    send_2, send_1, out_values, out_east, out_north, out_mask, out_rows, south, north, side
):
    lat = lax.axis_index("lat")
    top_block = lat == lax.axis_size("lat") - 1
    even = lax.rem(lat, 2) == 0
    even_lon = lax.rem(lax.axis_index("lon"), 2) == 0

    def part(q):
        rows = pl.ds(q * LEVELS, LEVELS)
        ob, oa, gb, ga = own_b[rows, :], own_a[rows, :], got_b[rows, :], got_a[rows, :]
        return ob, oa, jnp.where(even, gb, ga), jnp.where(even, ga, gb)

    flip = COLS - 1 - lanes(LEVELS)

    def own(q):
        ob, oa, _, _ = part(q)
        back = jnp.where(top_block, jnp.take_along_axis(oa, flip, axis=1), oa)
        return jnp.where(even, ob, back), jnp.where(even, oa, ob)

    def put(ref, half, slots, x):
        for j in slots:
            ref[pl.ds(half * 64 + j, LEVELS, stride=4), :] = x

    own_n, own_k = own(4)
    _, _, far_n, far_s = part(4)
    ghost_n = jnp.where(top_block, far_n, own_n * far_n)
    for m in range(2):
        own_t, own_bot = own(m)
        _, _, up, down = part(m)
        _, _, up_p, down_p = part(2 + m)
        gain_s = own_k * far_s * (down - own_bot)
        gain_n = own_n * (up - own_t)
        out_rows[pl.ds(m * LEVELS, LEVELS), :] = gain_s
        out_rows[pl.ds((2 + m) * LEVELS, LEVELS), :] = gain_n
        out_rows[pl.ds((4 + m) * LEVELS, LEVELS), :] = down_p - far_s * (down - own_bot)
        out_rows[pl.ds((6 + m) * LEVELS, LEVELS), :] = up_p - ghost_n * (up - own_t)
        put(south, m, (0, 3), down)
        put(south, m, (1, 2), gain_s)
        put(north, m, (0, 3), up)
        put(north, m, (1, 2), gain_n)
    out_rows[pl.ds(8 * LEVELS, LEVELS), :] = far_s
    _, _, up_e, down_e = part(5)
    put(side, 0, (0, 1), down_e)
    put(side, 0, (2, 3), far_s)
    put(side, 1, (0, 1, 2, 3), up_e)

    lane1 = lanes(1)
    slot1 = lax.rem(lane1, 4)
    turned_s = jnp.transpose(south[...])
    turned_n = jnp.transpose(north[...])
    turned_c = jnp.transpose(side[...])
    row_s = jnp.where(slot1 >= 2, turned_s[0:1, :], turned_s[COLS - 1 : COLS, :])
    row_n = jnp.where(slot1 >= 2, turned_n[0:1, :], turned_n[COLS - 1 : COLS, :])
    inner = (slot1 == 1) | (slot1 == 2)
    low_half = lane1 < 64
    first_c, last_c = turned_c[0:1, :], turned_c[COLS - 1 : COLS, :]
    face_s = jnp.where(low_half, last_c, turned(last_c, 64))
    coef_s = jnp.where(slot1 == 1, turned(last_c, -1), first_c)
    coef_s = jnp.where(low_half, coef_s, turned(coef_s, 64))
    face_n = jnp.where(low_half, turned(last_c, 64), last_c)
    mirrored = jnp.where(low_half, turned(first_c, 64), first_c)

    def extend(out, x, north_row, south_row):
        out[0:ROWS, :] = x[...]
        out[ROWS:PACKED, :] = jnp.zeros((PACKED - ROWS, COLS), F32)
        out[NORTH : NORTH + 1, :] = north_row
        out[SOUTH : SOUTH + 1, :] = south_row

    one = jnp.ones((1, COLS), F32)
    extend(out_values, values, row_n, row_s)
    out_values[0:1, :] = values[0:1, :] + jnp.where(inner, row_s, 0.0)
    out_values[ROWS - 1 : ROWS, :] = values[ROWS - 1 : ROWS, :] + jnp.where(inner, row_n, 0.0)
    extend(out_east, easts, jnp.where(top_block, one, face_n), face_s)
    extend(out_mask, masks, jnp.where(top_block, mirrored, one), one)
    extend(out_north, norths, jnp.zeros((1, COLS), F32), coef_s)
    slot = lax.rem(lanes(PACKED), 4)
    x = out_values[...]
    eastward = jnp.where(slot >= 2, turned(x, 2), out_east[...])
    westward = jnp.where(slot < 2, turned(x, -2), out_mask[...])
    send_1[...] = jnp.where(even_lon, eastward, westward)
    send_2[...] = jnp.where(even_lon, westward, eastward)


def second_step(u1_0, u1_1, mask, east, north, rows, out):
    u1 = (u1_0, u1_1)
    lane = lanes(ROWS)
    row = lax.broadcasted_iota(jnp.int32, (ROWS, COLS), 0)

    def line(q, l):
        return rows[pl.ds(q * LEVELS + l, 1), :]

    def level(l):
        k = mask[l].astype(F32)
        e_all = east[l]
        n = north[l]
        e = jnp.where(lane == COLS - 1, 0.0, e_all)
        w = jnp.where(lane == 0, 0.0, turned(e_all, 1))
        s = jnp.where(row == 0, line(8, l), slid(n, 1))
        for m in range(2):
            u = u1[m][l]
            u = jnp.where(row == 0, u + line(m, l), u)
            u = jnp.where(row == ROWS - 1, u + line(2 + m, l), u)
            u_n = jnp.where(row == ROWS - 1, line(6 + m, l), slid(u, -1))
            u_s = jnp.where(row == 0, line(4 + m, l), slid(u, 1))
            flux = e * (turned(u, -1) - u) - w * (u - turned(u, 1))
            flux = flux + n * (u_n - u) - s * (u - u_s)
            out[m, l] = k * (u + flux)

    for l in range(LEVELS):
        level(l)


def join_columns(u2, got_2, got_1, values, easts, norths, masks, out, gain, held, sem):
    even_lon = lax.rem(lax.axis_index("lon"), 2) == 0
    slot = lax.rem(lanes(PACKED), 4)
    is_east = slot == 1
    inner = is_east | (slot == 2)
    from_east = jnp.where(even_lon, got_1[...], got_2[...])
    from_west = jnp.where(even_lon, got_2[...], got_1[...])
    x, e, n, k = values[...], easts[...], norths[...], masks[...]
    own_0 = jnp.where(is_east, turned(x, 1), turned(x, -1))
    ghost_0 = jnp.where(is_east, from_east, from_west)
    ghost_1 = jnp.where(is_east, turned(from_east, 1), turned(from_west, -1))
    face = jnp.where(is_east, e * turned(from_east, -1), k * turned(from_west, 1))
    d = jnp.where(inner, face * (ghost_0 - own_0), 0.0)
    inside = jnp.where(is_east, turned(e, 1), e)
    s = slid(n, 1)
    change = d * (1.0 - inside - n - s) + face * (ghost_1 - x - d - d) + n * slid(d, -1) + s * slid(d, 1)
    beside = inside * d
    beside = jnp.where(slot == 0, turned(beside, -1), turned(beside, 1))
    gain[...] = k * jnp.where(inner, change, beside)

    lane = lanes(ROWS)
    edge = (lane < 2) | (lane >= COLS - 2)

    def copy(m, c):
        span = pl.ds(c * CHUNK, CHUNK)
        return pltpu.make_async_copy(held.at[m, span], out.at[m, span], sem.at[m, c])

    for c in range(LEVELS // CHUNK):
        for m in range(2):
            for l in range(c * CHUNK, (c + 1) * CHUNK):
                change = turned(gain[0:ROWS, :], 126 - 64 * m - 4 * l)
                held[m, l] = u2[m, l] + jnp.where(edge, change, 0.0)
            copy(m, c).start()
    for c in range(LEVELS // CHUNK):
        for m in range(2):
            copy(m, c).wait()


def struct(*shape):
    return jax.ShapeDtypeStruct(shape, F32)


def kernel(body, name, inputs, outputs, us, scratch=(), space=VMEM, limit=16):
    return pl.pallas_call(
        body,
        in_specs=[space] * inputs,
        out_specs=[VMEM if body is not join_columns else HBM] * len(outputs),
        out_shape=outputs,
        scratch_shapes=list(scratch),
        compiler_params=pltpu.CompilerParams(vmem_limit_bytes=int(limit * 1024 * 1024)),
        cost_estimate=pl.CostEstimate(flops=int(us * 4e6), bytes_accessed=int(us * 3e6), transcendentals=0),
        name=name,
    )


def local(noise, land_mask, east_coef, north_coef):
    n_lat, n_lon = lax.axis_size("lat"), lax.axis_size("lon")
    message = struct(6 * LEVELS, COLS)
    ends = pltpu.VMEM((2, LEVELS, 2, COLS), F32)
    scratch = [
        pltpu.VMEM((2, 2, LEVELS, 2, COLS), F32),
        pltpu.VMEM((2, LEVELS, 2, COLS), jnp.int32),
        ends,
        ends,
        pltpu.SemaphoreType.DMA((4, 2)),
    ]
    send_a, send_b = kernel(edge_rows, "edge_rows", 4, [message] * 2, 1, scratch, HBM, 53.5)(
        noise, land_mask, east_coef, north_coef
    )

    route_b = [(i, i ^ 1) for i in range(n_lat)]
    route_a = []
    for k in range(n_lon):
        for i in range(1, n_lat - 1):
            route_a.append((i * n_lon + k, (((i - 1) ^ 1) + 1) * n_lon + k))
        route_a.append(((n_lat - 1) * n_lon + k, n_lat * n_lon - 1 - k))
    got_a = lax.ppermute(send_a, ("lat", "lon"), route_a)
    got_b = lax.ppermute(send_b, "lat", route_b)

    whole, plane, packed = struct(2, LEVELS, ROWS, COLS), struct(ROWS, COLS), struct(PACKED, COLS)
    coef, levels = struct(LEVELS, ROWS, COLS), jax.ShapeDtypeStruct((LEVELS, ROWS, COLS), jnp.int32)
    outs = [coef] * 2 + [plane] * 4 + [coef] * 2 + [levels]
    scratch = [pltpu.VMEM((2 * LEVELS, ROWS, COLS), F32), pltpu.SemaphoreType.DMA((LEVELS // FETCH, 5))]
    u1_0, u1_1, *columns, east, north, mask = kernel(first_step, "first_step", 4, outs, 2, scratch, HBM, 51)(
        noise, land_mask, east_coef, north_coef
    )
    square = pltpu.VMEM((COLS, COLS), F32)
    send_2, send_1, *columns, rows = kernel(
        join_rows, "join_rows", 8, [packed] * 6 + [struct(9 * LEVELS, COLS)], 1, [square] * 3
    )(send_a, send_b, got_a, got_b, *columns)

    route_1 = [(k, k ^ 1) for k in range(n_lon)]
    route_2 = [(k, (((k + n_lon - 1) % n_lon ^ 1) + 1) % n_lon) for k in range(n_lon)]
    got_2 = lax.ppermute(send_2, "lon", route_2)
    got_1 = lax.ppermute(send_1, "lon", route_1)

    (u2,) = kernel(second_step, "second_step", 6, [whole], 2)(u1_0, u1_1, mask, east, north, rows)
    scratch = [pltpu.VMEM((PACKED, COLS), F32), pltpu.VMEM(whole.shape, F32), pltpu.SemaphoreType.DMA((2, LEVELS // CHUNK))]
    return kernel(join_columns, "join_columns", 7, [whole], 1, scratch)(u2, got_2, got_1, *columns)[0]


def solution(mesh):
    return jax.shard_map(
        local,
        mesh=mesh,
        in_specs=(
            P(None, None, "lat", "lon"),
            P(None, "lat", "lon"),
            P(None, "lat", "lon"),
            P(None, "lat", "lon"),
        ),
        out_specs=P(None, None, "lat", "lon"),
        check_vma=False,
    )
```

```python
import jax
import jax.numpy as jnp
from jax import lax
from jax.experimental import pallas as pl
from jax.experimental.pallas import tpu as pltpu
from jax.sharding import PartitionSpec as P


LEVELS, ROWS, COLS = 16, 64, 128
PACKED = 72
NORTH, SOUTH = 64, 71
F32 = jnp.float32
VMEM = pl.BlockSpec(memory_space=pltpu.VMEM)
HBM = pl.BlockSpec(memory_space=pltpu.HBM)


def lanes(rows):
    return lax.broadcasted_iota(jnp.int32, (rows, COLS), 1)


def turned(x, shift):
    return pltpu.roll(x, shift % COLS if isinstance(shift, int) else shift, 1)


def slid(x, shift):
    return pltpu.roll(x, shift % x.shape[0], 0)


def edge_rows(noise, mask, east, north, out_b, out_a, noise_at, mask_at, east_at, north_at, sem):
    copies = []
    for k, (whole, part) in enumerate(((noise, noise_at), (mask, mask_at), (east, east_at), (north, north_at))):
        for end in range(2):
            span = pl.ds(end * (ROWS - 2), 2)
            source = whole.at[:, :, span, :] if k == 0 else whole.at[:, span, :]
            copies.append(pltpu.make_async_copy(source, part.at[end], sem.at[k, end]))
    for copy in copies:
        copy.start()
    lat = lax.axis_index("lat")
    top_block = lat == lax.axis_size("lat") - 1
    even = lax.rem(lat, 2) == 0
    lane = lanes(LEVELS)

    def lateral(u, east, west):
        return east * (turned(u, -1) - u) - west * (u - turned(u, 1))

    def inner_faces(east):
        return jnp.where(lane == COLS - 1, 0.0, east), jnp.where(lane == 0, 0.0, turned(east, 1))

    for copy in copies:
        copy.wait()
    mask_t = mask_at[1, :, 1, :].astype(F32)
    mask_t2 = mask_at[1, :, 0, :].astype(F32)
    mask_b = mask_at[0, :, 0, :].astype(F32)
    mask_b2 = mask_at[0, :, 1, :].astype(F32)
    full_t, full_b = east_at[1, :, 1, :], east_at[0, :, 0, :]
    east_t, west_t = inner_faces(full_t)
    east_b, west_b = inner_faces(full_b)
    south_t = north_at[1, :, 0, :]
    north_b = north_at[0, :, 0, :]
    top, bottom = [], []
    top_p, bottom_p = [], []
    for m in range(2):
        u = noise_at[1, m, :, 1, :] * mask_t
        v = noise_at[1, m, :, 0, :] * mask_t2
        top.append(u)
        top_p.append(mask_t * (u + lateral(u, east_t, west_t) - south_t * (u - v)))
        u = noise_at[0, m, :, 0, :] * mask_b
        v = noise_at[0, m, :, 1, :] * mask_b2
        bottom.append(u)
        bottom_p.append(mask_b * (u + lateral(u, east_b, west_b) + north_b * (v - u)))
    top += top_p + [north_at[1, :, 1, :] * mask_t, full_t * mask_t]
    bottom += bottom_p + [mask_b, full_b * mask_b]
    flip = jnp.where(top_block, COLS - 1 - lane, lane)
    for q in range(6):
        rows = pl.ds(q * LEVELS, LEVELS)
        out_b[rows, :] = jnp.where(even, top[q], bottom[q])
        crossed = jnp.take_along_axis(top[q], flip, axis=1)
        out_a[rows, :] = jnp.where(even, bottom[q], crossed)


CHUNK = 4
FETCH = 8


def first_step(
    noise, mask, east, north, out_u0, out_u1, out_values, out_east, out_north, out_mask, held_east, held_north, held_mask, edges, sem
):
    out_u = (out_u0, out_u1)

    def copies(c, which):
        span = pl.ds(c * FETCH, FETCH)
        pairs = [(noise.at[0, span], out_u0.at[span]), (noise.at[1, span], out_u1.at[span])]
        pairs += [(mask.at[span], held_mask.at[span]), (east.at[span], held_east.at[span])]
        pairs += [(north.at[span], held_north.at[span])]
        return [pltpu.make_async_copy(*pairs[k], sem.at[c, k]) for k in which]

    fields, coefs = range(2), range(2, 5)
    for which in (coefs, fields):
        for c in range(LEVELS // FETCH):
            for copy in copies(c, which):
                copy.start()
    lane = lanes(ROWS)
    row = lax.broadcasted_iota(jnp.int32, (ROWS, COLS), 0)
    group = lane // 4

    def place(out, x, at):
        pltpu.store(out, turned(x, 4 * at + 2), mask=group == at)

    def level(l):
        k = held_mask[l].astype(F32)
        e_all = held_east[l]
        n_all = held_north[l]
        e = jnp.where(lane == COLS - 1, 0.0, e_all)
        w = jnp.where(lane == 0, 0.0, turned(e_all, 1))
        n = jnp.where(row == ROWS - 1, 0.0, n_all)
        s = jnp.where(row == 0, 0.0, slid(n_all, 1))
        for m in range(2):
            u = out_u[m][l] * k
            u_e, u_w = turned(u, -1), turned(u, 1)
            flux = e * (u_e - u) - w * (u - u_w)
            flux = flux + n * (slid(u, -1) - u) - s * (u - slid(u, 1))
            v = k * (u + flux)
            out_u[m][l] = v
            edges[m * LEVELS + l] = jnp.where(lane == COLS - 2, u_e, jnp.where(lane == 1, u_w, v))

    for c in range(LEVELS // FETCH):
        for copy in copies(c, coefs):
            copy.wait()
        for l in range(c * FETCH, (c + 1) * FETCH):
            k = held_mask[l].astype(F32)
            place(out_east, held_east[l] * k, l)
            place(out_north, held_north[l], l)
            place(out_mask, k, l)
    for c in range(LEVELS // FETCH):
        for copy in copies(c, fields):
            copy.wait()
        for l in range(c * FETCH, (c + 1) * FETCH):
            level(l)
    for g in range(2 * LEVELS):
        place(out_values, edges[g], g)
    for out in (out_east, out_north, out_mask):
        out[...] = jnp.where(lane < 64, out[...], turned(out[...], 64))


def join_rows(
    own_b, own_a, got_b, got_a, values, easts, norths, masks,
    send_2, send_1, out_values, out_east, out_north, out_mask, out_rows, south, north, side
):
    lat = lax.axis_index("lat")
    top_block = lat == lax.axis_size("lat") - 1
    even = lax.rem(lat, 2) == 0
    even_lon = lax.rem(lax.axis_index("lon"), 2) == 0

    def part(q):
        rows = pl.ds(q * LEVELS, LEVELS)
        ob, oa, gb, ga = own_b[rows, :], own_a[rows, :], got_b[rows, :], got_a[rows, :]
        return ob, oa, jnp.where(even, gb, ga), jnp.where(even, ga, gb)

    flip = COLS - 1 - lanes(LEVELS)

    def own(q):
        ob, oa, _, _ = part(q)
        back = jnp.where(top_block, jnp.take_along_axis(oa, flip, axis=1), oa)
        return jnp.where(even, ob, back), jnp.where(even, oa, ob)

    def put(ref, half, slots, x):
        for j in slots:
            ref[pl.ds(half * 64 + j, LEVELS, stride=4), :] = x

    own_n, own_k = own(4)
    _, _, far_n, far_s = part(4)
    ghost_n = jnp.where(top_block, far_n, own_n * far_n)
    for m in range(2):
        own_t, own_bot = own(m)
        _, _, up, down = part(m)
        _, _, up_p, down_p = part(2 + m)
        gain_s = own_k * far_s * (down - own_bot)
        gain_n = own_n * (up - own_t)
        out_rows[pl.ds(m * LEVELS, LEVELS), :] = gain_s
        out_rows[pl.ds((2 + m) * LEVELS, LEVELS), :] = gain_n
        out_rows[pl.ds((4 + m) * LEVELS, LEVELS), :] = down_p - far_s * (down - own_bot)
        out_rows[pl.ds((6 + m) * LEVELS, LEVELS), :] = up_p - ghost_n * (up - own_t)
        put(south, m, (0, 3), down)
        put(south, m, (1, 2), gain_s)
        put(north, m, (0, 3), up)
        put(north, m, (1, 2), gain_n)
    out_rows[pl.ds(8 * LEVELS, LEVELS), :] = far_s
    _, _, up_e, down_e = part(5)
    put(side, 0, (0, 1), down_e)
    put(side, 0, (2, 3), far_s)
    put(side, 1, (0, 1, 2, 3), up_e)

    lane1 = lanes(1)
    slot1 = lax.rem(lane1, 4)
    turned_s = jnp.transpose(south[...])
    turned_n = jnp.transpose(north[...])
    turned_c = jnp.transpose(side[...])
    row_s = jnp.where(slot1 >= 2, turned_s[0:1, :], turned_s[COLS - 1 : COLS, :])
    row_n = jnp.where(slot1 >= 2, turned_n[0:1, :], turned_n[COLS - 1 : COLS, :])
    inner = (slot1 == 1) | (slot1 == 2)
    low_half = lane1 < 64
    first_c, last_c = turned_c[0:1, :], turned_c[COLS - 1 : COLS, :]
    face_s = jnp.where(low_half, last_c, turned(last_c, 64))
    coef_s = jnp.where(slot1 == 1, turned(last_c, -1), first_c)
    coef_s = jnp.where(low_half, coef_s, turned(coef_s, 64))
    face_n = jnp.where(low_half, turned(last_c, 64), last_c)
    mirrored = jnp.where(low_half, turned(first_c, 64), first_c)

    def extend(out, x, north_row, south_row):
        out[0:ROWS, :] = x[...]
        out[ROWS:PACKED, :] = jnp.zeros((PACKED - ROWS, COLS), F32)
        out[NORTH : NORTH + 1, :] = north_row
        out[SOUTH : SOUTH + 1, :] = south_row

    one = jnp.ones((1, COLS), F32)
    extend(out_values, values, row_n, row_s)
    out_values[0:1, :] = values[0:1, :] + jnp.where(inner, row_s, 0.0)
    out_values[ROWS - 1 : ROWS, :] = values[ROWS - 1 : ROWS, :] + jnp.where(inner, row_n, 0.0)
    extend(out_east, easts, jnp.where(top_block, one, face_n), face_s)
    extend(out_mask, masks, jnp.where(top_block, mirrored, one), one)
    extend(out_north, norths, jnp.zeros((1, COLS), F32), coef_s)
    slot = lax.rem(lanes(PACKED), 4)
    x = out_values[...]
    eastward = jnp.where(slot >= 2, turned(x, 2), out_east[...])
    westward = jnp.where(slot < 2, turned(x, -2), out_mask[...])
    send_1[...] = jnp.where(even_lon, eastward, westward)
    send_2[...] = jnp.where(even_lon, westward, eastward)


def second_step(u1_0, u1_1, mask, east, north, rows, out):
    u1 = (u1_0, u1_1)
    lane = lanes(ROWS)
    row = lax.broadcasted_iota(jnp.int32, (ROWS, COLS), 0)

    def line(q, l):
        return rows[pl.ds(q * LEVELS + l, 1), :]

    def level(l):
        k = mask[l].astype(F32)
        e_all = east[l]
        n = north[l]
        e = jnp.where(lane == COLS - 1, 0.0, e_all)
        w = jnp.where(lane == 0, 0.0, turned(e_all, 1))
        s = jnp.where(row == 0, line(8, l), slid(n, 1))
        for m in range(2):
            u = u1[m][l]
            u = jnp.where(row == 0, u + line(m, l), u)
            u = jnp.where(row == ROWS - 1, u + line(2 + m, l), u)
            u_n = jnp.where(row == ROWS - 1, line(6 + m, l), slid(u, -1))
            u_s = jnp.where(row == 0, line(4 + m, l), slid(u, 1))
            flux = e * (turned(u, -1) - u) - w * (u - turned(u, 1))
            flux = flux + n * (u_n - u) - s * (u - u_s)
            out[m, l] = k * (u + flux)

    for l in range(LEVELS):
        level(l)


def join_columns(u2, got_2, got_1, values, easts, norths, masks, out, gain, held, sem):
    even_lon = lax.rem(lax.axis_index("lon"), 2) == 0
    slot = lax.rem(lanes(PACKED), 4)
    is_east = slot == 1
    inner = is_east | (slot == 2)
    from_east = jnp.where(even_lon, got_1[...], got_2[...])
    from_west = jnp.where(even_lon, got_2[...], got_1[...])
    x, e, n, k = values[...], easts[...], norths[...], masks[...]
    own_0 = jnp.where(is_east, turned(x, 1), turned(x, -1))
    ghost_0 = jnp.where(is_east, from_east, from_west)
    ghost_1 = jnp.where(is_east, turned(from_east, 1), turned(from_west, -1))
    face = jnp.where(is_east, e * turned(from_east, -1), k * turned(from_west, 1))
    d = jnp.where(inner, face * (ghost_0 - own_0), 0.0)
    inside = jnp.where(is_east, turned(e, 1), e)
    s = slid(n, 1)
    change = d * (1.0 - inside - n - s) + face * (ghost_1 - x - d - d) + n * slid(d, -1) + s * slid(d, 1)
    beside = inside * d
    beside = jnp.where(slot == 0, turned(beside, -1), turned(beside, 1))
    gain[...] = k * jnp.where(inner, change, beside)

    lane = lanes(ROWS)
    edge = (lane < 2) | (lane >= COLS - 2)

    def copy(m, c):
        span = pl.ds(c * CHUNK, CHUNK)
        return pltpu.make_async_copy(held.at[m, span], out.at[m, span], sem.at[m, c])

    for c in range(LEVELS // CHUNK):
        for m in range(2):
            for l in range(c * CHUNK, (c + 1) * CHUNK):
                change = turned(gain[0:ROWS, :], 126 - 64 * m - 4 * l)
                held[m, l] = u2[m, l] + jnp.where(edge, change, 0.0)
            copy(m, c).start()
    for c in range(LEVELS // CHUNK):
        for m in range(2):
            copy(m, c).wait()


def struct(*shape):
    return jax.ShapeDtypeStruct(shape, F32)


def kernel(body, name, inputs, outputs, us, scratch=(), space=VMEM, limit=16):
    return pl.pallas_call(
        body,
        in_specs=[space] * inputs,
        out_specs=[VMEM if body is not join_columns else HBM] * len(outputs),
        out_shape=outputs,
        scratch_shapes=list(scratch),
        compiler_params=pltpu.CompilerParams(vmem_limit_bytes=int(limit * 1024 * 1024)),
        cost_estimate=pl.CostEstimate(flops=int(us * 4e6), bytes_accessed=int(us * 3e6), transcendentals=0),
        name=name,
    )


def local(noise, land_mask, east_coef, north_coef):
    n_lat, n_lon = lax.axis_size("lat"), lax.axis_size("lon")
    message = struct(6 * LEVELS, COLS)
    ends = pltpu.VMEM((2, LEVELS, 2, COLS), F32)
    scratch = [
        pltpu.VMEM((2, 2, LEVELS, 2, COLS), F32),
        pltpu.VMEM((2, LEVELS, 2, COLS), jnp.int32),
        ends,
        ends,
        pltpu.SemaphoreType.DMA((4, 2)),
    ]
    send_b, send_a = kernel(edge_rows, "edge_rows", 4, [message] * 2, 1, scratch, HBM, 53.5)(
        noise, land_mask, east_coef, north_coef
    )

    route_b = [(i, i ^ 1) for i in range(n_lat)]
    route_a = []
    for k in range(n_lon):
        for i in range(1, n_lat - 1):
            route_a.append((i * n_lon + k, (((i - 1) ^ 1) + 1) * n_lon + k))
        route_a.append(((n_lat - 1) * n_lon + k, n_lat * n_lon - 1 - k))
    got_a = lax.ppermute(send_a, ("lat", "lon"), route_a)
    got_b = lax.ppermute(send_b, "lat", route_b)

    whole, plane, packed = struct(2, LEVELS, ROWS, COLS), struct(ROWS, COLS), struct(PACKED, COLS)
    coef, levels = struct(LEVELS, ROWS, COLS), jax.ShapeDtypeStruct((LEVELS, ROWS, COLS), jnp.int32)
    outs = [coef] * 2 + [plane] * 4 + [coef] * 2 + [levels]
    scratch = [pltpu.VMEM((2 * LEVELS, ROWS, COLS), F32), pltpu.SemaphoreType.DMA((LEVELS // FETCH, 5))]
    u1_0, u1_1, *columns, east, north, mask = kernel(first_step, "first_step", 4, outs, 2, scratch, HBM, 51)(
        noise, land_mask, east_coef, north_coef
    )
    square = pltpu.VMEM((COLS, COLS), F32)
    send_2, send_1, *columns, rows = kernel(
        join_rows, "join_rows", 8, [packed] * 6 + [struct(9 * LEVELS, COLS)], 1, [square] * 3
    )(send_b, send_a, got_b, got_a, *columns)

    route_1 = [(k, k ^ 1) for k in range(n_lon)]
    route_2 = [(k, (((k + n_lon - 1) % n_lon ^ 1) + 1) % n_lon) for k in range(n_lon)]
    got_2 = lax.ppermute(send_2, "lon", route_2)
    got_1 = lax.ppermute(send_1, "lon", route_1)

    (u2,) = kernel(second_step, "second_step", 6, [whole], 2)(u1_0, u1_1, mask, east, north, rows)
    scratch = [pltpu.VMEM((PACKED, COLS), F32), pltpu.VMEM(whole.shape, F32), pltpu.SemaphoreType.DMA((2, LEVELS // CHUNK))]
    return kernel(join_columns, "join_columns", 7, [whole], 1, scratch)(u2, got_2, got_1, *columns)[0]


def solution(mesh):
    return jax.shard_map(
        local,
        mesh=mesh,
        in_specs=(
            P(None, None, "lat", "lon"),
            P(None, "lat", "lon"),
            P(None, "lat", "lon"),
            P(None, "lat", "lon"),
        ),
        out_specs=P(None, None, "lat", "lon"),
        check_vma=False,
    )
```

```python
import jax
import jax.numpy as jnp
from jax import lax
from jax.experimental import pallas as pl
from jax.experimental.pallas import tpu as pltpu
from jax.sharding import PartitionSpec as P


LEVELS, ROWS, COLS = 16, 64, 128
PACKED = 72
NORTH, SOUTH = 64, 71
F32 = jnp.float32
VMEM = pl.BlockSpec(memory_space=pltpu.VMEM)
HBM = pl.BlockSpec(memory_space=pltpu.HBM)


def lanes(rows):
    return lax.broadcasted_iota(jnp.int32, (rows, COLS), 1)


def turned(x, shift):
    return pltpu.roll(x, shift % COLS if isinstance(shift, int) else shift, 1)


def slid(x, shift):
    return pltpu.roll(x, shift % x.shape[0], 0)


def edge_rows(noise, mask, east, north, out_b, out_a, noise_at, mask_at, east_at, north_at, sem):
    copies = []
    for k, (whole, part) in enumerate(((noise, noise_at), (mask, mask_at), (east, east_at), (north, north_at))):
        for end in range(2):
            span = pl.ds(end * (ROWS - 2), 2)
            source = whole.at[:, :, span, :] if k == 0 else whole.at[:, span, :]
            copies.append(pltpu.make_async_copy(source, part.at[end], sem.at[k, end]))
    for copy in copies:
        copy.start()
    lat = lax.axis_index("lat")
    top_block = lat == lax.axis_size("lat") - 1
    even = lax.rem(lat, 2) == 0
    lane = lanes(LEVELS)

    def lateral(u, east, west):
        return east * (turned(u, -1) - u) - west * (u - turned(u, 1))

    def inner_faces(east):
        return jnp.where(lane == COLS - 1, 0.0, east), jnp.where(lane == 0, 0.0, turned(east, 1))

    for copy in copies:
        copy.wait()
    mask_t = mask_at[1, :, 1, :].astype(F32)
    mask_t2 = mask_at[1, :, 0, :].astype(F32)
    mask_b = mask_at[0, :, 0, :].astype(F32)
    mask_b2 = mask_at[0, :, 1, :].astype(F32)
    full_t, full_b = east_at[1, :, 1, :], east_at[0, :, 0, :]
    east_t, west_t = inner_faces(full_t)
    east_b, west_b = inner_faces(full_b)
    south_t = north_at[1, :, 0, :]
    north_b = north_at[0, :, 0, :]
    top, bottom = [], []
    top_p, bottom_p = [], []
    for m in range(2):
        u = noise_at[1, m, :, 1, :] * mask_t
        v = noise_at[1, m, :, 0, :] * mask_t2
        top.append(u)
        top_p.append(mask_t * (u + lateral(u, east_t, west_t) - south_t * (u - v)))
        u = noise_at[0, m, :, 0, :] * mask_b
        v = noise_at[0, m, :, 1, :] * mask_b2
        bottom.append(u)
        bottom_p.append(mask_b * (u + lateral(u, east_b, west_b) + north_b * (v - u)))
    top += top_p + [north_at[1, :, 1, :] * mask_t]
    bottom += bottom_p + [mask_b]
    flip = jnp.where(top_block, COLS - 1 - lane, lane)
    def last_column(x):
        level = lax.broadcasted_iota(jnp.int32, (LEVELS, COLS), 0)
        return jnp.sum(jnp.where(lane == level, x[:, COLS - 1 :], 0.0), axis=0, keepdims=True)

    face_t, face_b = last_column(full_t * mask_t), last_column(full_b * mask_b)
    tail = pl.ds(5 * LEVELS, 8)
    out_b[tail, :] = jnp.broadcast_to(jnp.where(even, face_t, face_b), (8, COLS))
    out_a[tail, :] = jnp.broadcast_to(jnp.where(even, face_b, face_t), (8, COLS))
    for q in range(5):
        rows = pl.ds(q * LEVELS, LEVELS)
        out_b[rows, :] = jnp.where(even, top[q], bottom[q])
        crossed = jnp.take_along_axis(top[q], flip, axis=1)
        out_a[rows, :] = jnp.where(even, bottom[q], crossed)


CHUNK = 4
FETCH = 8


def first_step(
    noise, mask, east, north, out_u0, out_u1, out_values, out_east, out_north, out_mask, held_east, held_north, held_mask, edges, sem
):
    out_u = (out_u0, out_u1)

    def copies(c, which):
        span = pl.ds(c * FETCH, FETCH)
        pairs = [(noise.at[0, span], out_u0.at[span]), (noise.at[1, span], out_u1.at[span])]
        pairs += [(mask.at[span], held_mask.at[span]), (east.at[span], held_east.at[span])]
        pairs += [(north.at[span], held_north.at[span])]
        return [pltpu.make_async_copy(*pairs[k], sem.at[c, k]) for k in which]

    fields, coefs = range(2), range(2, 5)
    for which in (coefs, fields):
        for c in range(LEVELS // FETCH):
            for copy in copies(c, which):
                copy.start()
    lane = lanes(ROWS)
    row = lax.broadcasted_iota(jnp.int32, (ROWS, COLS), 0)
    group = lane // 4

    def place(out, x, at):
        pltpu.store(out, turned(x, 4 * at + 2), mask=group == at)

    def level(l):
        k = held_mask[l].astype(F32)
        e_all = held_east[l]
        n_all = held_north[l]
        e = jnp.where(lane == COLS - 1, 0.0, e_all)
        w = jnp.where(lane == 0, 0.0, turned(e_all, 1))
        n = jnp.where(row == ROWS - 1, 0.0, n_all)
        s = jnp.where(row == 0, 0.0, slid(n_all, 1))
        for m in range(2):
            u = out_u[m][l] * k
            u_e, u_w = turned(u, -1), turned(u, 1)
            flux = e * (u_e - u) - w * (u - u_w)
            flux = flux + n * (slid(u, -1) - u) - s * (u - slid(u, 1))
            v = k * (u + flux)
            out_u[m][l] = v
            edges[m * LEVELS + l] = jnp.where(lane == COLS - 2, u_e, jnp.where(lane == 1, u_w, v))

    for c in range(LEVELS // FETCH):
        for copy in copies(c, coefs):
            copy.wait()
        for l in range(c * FETCH, (c + 1) * FETCH):
            k = held_mask[l].astype(F32)
            place(out_east, held_east[l] * k, l)
            place(out_north, held_north[l], l)
            place(out_mask, k, l)
    for c in range(LEVELS // FETCH):
        for copy in copies(c, fields):
            copy.wait()
        for l in range(c * FETCH, (c + 1) * FETCH):
            level(l)
    for g in range(2 * LEVELS):
        place(out_values, edges[g], g)
    for out in (out_east, out_north, out_mask):
        out[...] = jnp.where(lane < 64, out[...], turned(out[...], 64))


def join_rows(
    own_b, own_a, got_b, got_a, values, easts, norths, masks,
    send_2, send_1, out_values, out_east, out_north, out_mask, out_rows, south, north, side
):
    lat = lax.axis_index("lat")
    top_block = lat == lax.axis_size("lat") - 1
    even = lax.rem(lat, 2) == 0
    even_lon = lax.rem(lax.axis_index("lon"), 2) == 0

    def part(q):
        rows = pl.ds(q * LEVELS, LEVELS)
        ob, oa, gb, ga = own_b[rows, :], own_a[rows, :], got_b[rows, :], got_a[rows, :]
        return ob, oa, jnp.where(even, gb, ga), jnp.where(even, ga, gb)

    flip = COLS - 1 - lanes(LEVELS)

    def own(q):
        ob, oa, _, _ = part(q)
        back = jnp.where(top_block, jnp.take_along_axis(oa, flip, axis=1), oa)
        return jnp.where(even, ob, back), jnp.where(even, oa, ob)

    def put(ref, half, slots, x):
        for j in slots:
            ref[pl.ds(half * 64 + j, LEVELS, stride=4), :] = x

    own_n, own_k = own(4)
    _, _, far_n, far_s = part(4)
    ghost_n = jnp.where(top_block, far_n, own_n * far_n)
    for m in range(2):
        own_t, own_bot = own(m)
        _, _, up, down = part(m)
        _, _, up_p, down_p = part(2 + m)
        gain_s = own_k * far_s * (down - own_bot)
        gain_n = own_n * (up - own_t)
        out_rows[pl.ds(m * LEVELS, LEVELS), :] = gain_s
        out_rows[pl.ds((2 + m) * LEVELS, LEVELS), :] = gain_n
        out_rows[pl.ds((4 + m) * LEVELS, LEVELS), :] = down_p - far_s * (down - own_bot)
        out_rows[pl.ds((6 + m) * LEVELS, LEVELS), :] = up_p - ghost_n * (up - own_t)
        put(south, m, (0, 3), down)
        put(south, m, (1, 2), gain_s)
        put(north, m, (0, 3), up)
        put(north, m, (1, 2), gain_n)
    out_rows[pl.ds(8 * LEVELS, LEVELS), :] = far_s
    put(side, 0, (2, 3), far_s)
    tail = pl.ds(5 * LEVELS, 8)
    spread = lax.rem(lanes(8), 64) // 4
    up_e = jnp.take_along_axis(jnp.where(even, got_b[tail, :], got_a[tail, :]), spread, axis=1)
    down_e = jnp.take_along_axis(jnp.where(even, got_a[tail, :], got_b[tail, :]), spread, axis=1)

    lane1 = lanes(1)
    slot1 = lax.rem(lane1, 4)
    turned_s = jnp.transpose(south[...])
    turned_n = jnp.transpose(north[...])
    turned_c = jnp.transpose(side[...])
    row_s = jnp.where(slot1 >= 2, turned_s[0:1, :], turned_s[COLS - 1 : COLS, :])
    row_n = jnp.where(slot1 >= 2, turned_n[0:1, :], turned_n[COLS - 1 : COLS, :])
    inner = (slot1 == 1) | (slot1 == 2)
    low_half = lane1 < 64
    first_c, last_c = turned_c[0:1, :], turned_c[COLS - 1 : COLS, :]
    face_s, face_n = down_e[0:1, :], up_e[0:1, :]
    coef_s = jnp.where(slot1 == 1, turned(last_c, -1), first_c)
    coef_s = jnp.where(low_half, coef_s, turned(coef_s, 64))

    def extend(out, x, north_row, south_row):
        out[0:ROWS, :] = x[...]
        out[ROWS:PACKED, :] = jnp.zeros((PACKED - ROWS, COLS), F32)
        out[NORTH : NORTH + 1, :] = north_row
        out[SOUTH : SOUTH + 1, :] = south_row

    one = jnp.ones((1, COLS), F32)
    extend(out_values, values, row_n, row_s)
    out_values[0:1, :] = values[0:1, :] + jnp.where(inner, row_s, 0.0)
    out_values[ROWS - 1 : ROWS, :] = values[ROWS - 1 : ROWS, :] + jnp.where(inner, row_n, 0.0)
    extend(out_east, easts, jnp.where(top_block, one, face_n), face_s)
    extend(out_mask, masks, jnp.where(top_block, face_n, one), one)
    extend(out_north, norths, jnp.zeros((1, COLS), F32), coef_s)
    slot = lax.rem(lanes(PACKED), 4)
    x = out_values[...]
    eastward = jnp.where(slot >= 2, turned(x, 2), out_east[...])
    westward = jnp.where(slot < 2, turned(x, -2), out_mask[...])
    send_1[...] = jnp.where(even_lon, eastward, westward)
    send_2[...] = jnp.where(even_lon, westward, eastward)


def second_step(u1_0, u1_1, mask, east, north, rows, out):
    u1 = (u1_0, u1_1)
    lane = lanes(ROWS)
    row = lax.broadcasted_iota(jnp.int32, (ROWS, COLS), 0)

    def line(q, l):
        return rows[pl.ds(q * LEVELS + l, 1), :]

    def level(l):
        k = mask[l].astype(F32)
        e_all = east[l]
        n = north[l]
        e = jnp.where(lane == COLS - 1, 0.0, e_all)
        w = jnp.where(lane == 0, 0.0, turned(e_all, 1))
        s = jnp.where(row == 0, line(8, l), slid(n, 1))
        for m in range(2):
            u = u1[m][l]
            u = jnp.where(row == 0, u + line(m, l), u)
            u = jnp.where(row == ROWS - 1, u + line(2 + m, l), u)
            u_n = jnp.where(row == ROWS - 1, line(6 + m, l), slid(u, -1))
            u_s = jnp.where(row == 0, line(4 + m, l), slid(u, 1))
            flux = e * (turned(u, -1) - u) - w * (u - turned(u, 1))
            flux = flux + n * (u_n - u) - s * (u - u_s)
            out[m, l] = k * (u + flux)

    for l in range(LEVELS):
        level(l)


def join_columns(u2, got_2, got_1, values, easts, norths, masks, out, gain, held, sem):
    even_lon = lax.rem(lax.axis_index("lon"), 2) == 0
    slot = lax.rem(lanes(PACKED), 4)
    is_east = slot == 1
    inner = is_east | (slot == 2)
    from_east = jnp.where(even_lon, got_1[...], got_2[...])
    from_west = jnp.where(even_lon, got_2[...], got_1[...])
    x, e, n, k = values[...], easts[...], norths[...], masks[...]
    own_0 = jnp.where(is_east, turned(x, 1), turned(x, -1))
    ghost_0 = jnp.where(is_east, from_east, from_west)
    ghost_1 = jnp.where(is_east, turned(from_east, 1), turned(from_west, -1))
    face = jnp.where(is_east, e * turned(from_east, -1), k * turned(from_west, 1))
    d = jnp.where(inner, face * (ghost_0 - own_0), 0.0)
    inside = jnp.where(is_east, turned(e, 1), e)
    s = slid(n, 1)
    change = d * (1.0 - inside - n - s) + face * (ghost_1 - x - d - d) + n * slid(d, -1) + s * slid(d, 1)
    beside = inside * d
    beside = jnp.where(slot == 0, turned(beside, -1), turned(beside, 1))
    gain[...] = k * jnp.where(inner, change, beside)

    lane = lanes(ROWS)
    edge = (lane < 2) | (lane >= COLS - 2)

    def copy(m, c):
        span = pl.ds(c * CHUNK, CHUNK)
        return pltpu.make_async_copy(held.at[m, span], out.at[m, span], sem.at[m, c])

    for c in range(LEVELS // CHUNK):
        for m in range(2):
            for l in range(c * CHUNK, (c + 1) * CHUNK):
                change = turned(gain[0:ROWS, :], 126 - 64 * m - 4 * l)
                held[m, l] = u2[m, l] + jnp.where(edge, change, 0.0)
            copy(m, c).start()
    for c in range(LEVELS // CHUNK):
        for m in range(2):
            copy(m, c).wait()


def struct(*shape):
    return jax.ShapeDtypeStruct(shape, F32)


def kernel(body, name, inputs, outputs, us, scratch=(), space=VMEM, limit=16):
    return pl.pallas_call(
        body,
        in_specs=[space] * inputs,
        out_specs=[VMEM if body is not join_columns else HBM] * len(outputs),
        out_shape=outputs,
        scratch_shapes=list(scratch),
        compiler_params=pltpu.CompilerParams(vmem_limit_bytes=int(limit * 1024 * 1024)),
        cost_estimate=pl.CostEstimate(flops=int(us * 4e6), bytes_accessed=int(us * 3e6), transcendentals=0),
        name=name,
    )


def local(noise, land_mask, east_coef, north_coef):
    n_lat, n_lon = lax.axis_size("lat"), lax.axis_size("lon")
    message = struct(5 * LEVELS + 8, COLS)
    ends = pltpu.VMEM((2, LEVELS, 2, COLS), F32)
    scratch = [
        pltpu.VMEM((2, 2, LEVELS, 2, COLS), F32),
        pltpu.VMEM((2, LEVELS, 2, COLS), jnp.int32),
        ends,
        ends,
        pltpu.SemaphoreType.DMA((4, 2)),
    ]
    send_b, send_a = kernel(edge_rows, "edge_rows", 4, [message] * 2, 1, scratch, HBM, 53.5)(
        noise, land_mask, east_coef, north_coef
    )

    route_b = [(i, i ^ 1) for i in range(n_lat)]
    route_a = []
    for k in range(n_lon):
        for i in range(1, n_lat - 1):
            route_a.append((i * n_lon + k, (((i - 1) ^ 1) + 1) * n_lon + k))
        route_a.append(((n_lat - 1) * n_lon + k, n_lat * n_lon - 1 - k))
    got_a = lax.ppermute(send_a, ("lat", "lon"), route_a)
    got_b = lax.ppermute(send_b, "lat", route_b)

    whole, plane, packed = struct(2, LEVELS, ROWS, COLS), struct(ROWS, COLS), struct(PACKED, COLS)
    coef, levels = struct(LEVELS, ROWS, COLS), jax.ShapeDtypeStruct((LEVELS, ROWS, COLS), jnp.int32)
    outs = [coef] * 2 + [plane] * 4 + [coef] * 2 + [levels]
    scratch = [pltpu.VMEM((2 * LEVELS, ROWS, COLS), F32), pltpu.SemaphoreType.DMA((LEVELS // FETCH, 5))]
    u1_0, u1_1, *columns, east, north, mask = kernel(first_step, "first_step", 4, outs, 2, scratch, HBM, 51)(
        noise, land_mask, east_coef, north_coef
    )
    square = pltpu.VMEM((COLS, COLS), F32)
    send_2, send_1, *columns, rows = kernel(
        join_rows, "join_rows", 8, [packed] * 6 + [struct(9 * LEVELS, COLS)], 1, [square] * 3
    )(send_b, send_a, got_b, got_a, *columns)

    route_1 = [(k, k ^ 1) for k in range(n_lon)]
    route_2 = [(k, (((k + n_lon - 1) % n_lon ^ 1) + 1) % n_lon) for k in range(n_lon)]
    got_2 = lax.ppermute(send_2, "lon", route_2)
    got_1 = lax.ppermute(send_1, "lon", route_1)

    (u2,) = kernel(second_step, "second_step", 6, [whole], 2)(u1_0, u1_1, mask, east, north, rows)
    scratch = [pltpu.VMEM((PACKED, COLS), F32), pltpu.VMEM(whole.shape, F32), pltpu.SemaphoreType.DMA((2, LEVELS // CHUNK))]
    return kernel(join_columns, "join_columns", 7, [whole], 1, scratch)(u2, got_2, got_1, *columns)[0]


def solution(mesh):
    return jax.shard_map(
        local,
        mesh=mesh,
        in_specs=(
            P(None, None, "lat", "lon"),
            P(None, "lat", "lon"),
            P(None, "lat", "lon"),
            P(None, "lat", "lon"),
        ),
        out_specs=P(None, None, "lat", "lon"),
        check_vma=False,
    )
```

```python
import jax
import jax.numpy as jnp
from jax import lax
from jax.experimental import pallas as pl
from jax.experimental.pallas import tpu as pltpu
from jax.sharding import PartitionSpec as P


LEVELS, ROWS, COLS = 16, 64, 128
PACKED = 72
NORTH, SOUTH = 64, 71
F32 = jnp.float32
VMEM = pl.BlockSpec(memory_space=pltpu.VMEM)
HBM = pl.BlockSpec(memory_space=pltpu.HBM)


def lanes(rows):
    return lax.broadcasted_iota(jnp.int32, (rows, COLS), 1)


def turned(x, shift):
    return pltpu.roll(x, shift % COLS if isinstance(shift, int) else shift, 1)


def slid(x, shift):
    return pltpu.roll(x, shift % x.shape[0], 0)


def edge_rows(noise, mask, east, north, out_b, out_a, noise_at, mask_at, east_at, north_at, sem):
    copies = []
    for k, (whole, part) in enumerate(((noise, noise_at), (mask, mask_at), (east, east_at), (north, north_at))):
        for end in range(2):
            span = pl.ds(end * (ROWS - 2), 2)
            source = whole.at[:, :, span, :] if k == 0 else whole.at[:, span, :]
            copies.append(pltpu.make_async_copy(source, part.at[end], sem.at[k, end]))
    for copy in copies:
        copy.start()
    lat = lax.axis_index("lat")
    top_block = lat == lax.axis_size("lat") - 1
    even = lax.rem(lat, 2) == 0
    lane = lanes(LEVELS)

    def lateral(u, east, west):
        return east * (turned(u, -1) - u) - west * (u - turned(u, 1))

    def inner_faces(east):
        return jnp.where(lane == COLS - 1, 0.0, east), jnp.where(lane == 0, 0.0, turned(east, 1))

    for copy in copies:
        copy.wait()
    mask_t = mask_at[1, :, 1, :].astype(F32)
    mask_t2 = mask_at[1, :, 0, :].astype(F32)
    mask_b = mask_at[0, :, 0, :].astype(F32)
    mask_b2 = mask_at[0, :, 1, :].astype(F32)
    full_t, full_b = east_at[1, :, 1, :], east_at[0, :, 0, :]
    east_t, west_t = inner_faces(full_t)
    east_b, west_b = inner_faces(full_b)
    south_t = north_at[1, :, 0, :]
    north_b = north_at[0, :, 0, :]
    top, bottom = [], []
    top_p, bottom_p = [], []
    for m in range(2):
        u = noise_at[1, m, :, 1, :] * mask_t
        v = noise_at[1, m, :, 0, :] * mask_t2
        top.append(u)
        top_p.append(mask_t * (u + lateral(u, east_t, west_t) - south_t * (u - v)))
        u = noise_at[0, m, :, 0, :] * mask_b
        v = noise_at[0, m, :, 1, :] * mask_b2
        bottom.append(u)
        bottom_p.append(mask_b * (u + lateral(u, east_b, west_b) + north_b * (v - u)))
    top += top_p + [north_at[1, :, 1, :] * mask_t]
    bottom += bottom_p + [mask_b]
    flip = jnp.where(top_block, COLS - 1 - lane, lane)
    def last_column(x):
        level = lax.broadcasted_iota(jnp.int32, (LEVELS, COLS), 0)
        return jnp.sum(jnp.where(lane == level, x[:, COLS - 1 :], 0.0), axis=0, keepdims=True)

    face_t, face_b = last_column(full_t * mask_t), last_column(full_b * mask_b)
    tail = pl.ds(5 * LEVELS, 8)
    out_b[tail, :] = jnp.broadcast_to(jnp.where(even, face_t, face_b), (8, COLS))
    out_a[tail, :] = jnp.broadcast_to(jnp.where(even, face_b, face_t), (8, COLS))
    for q in range(5):
        rows = pl.ds(q * LEVELS, LEVELS)
        out_b[rows, :] = jnp.where(even, top[q], bottom[q])
        crossed = jnp.take_along_axis(top[q], flip, axis=1)
        out_a[rows, :] = jnp.where(even, bottom[q], crossed)


CHUNK = 4
FETCH = 8


def first_step(
    noise, mask, east, north, out_u0, out_u1, out_values, out_east, out_north, out_mask, held_east, held_north, held_mask, edges, sem
):
    out_u = (out_u0, out_u1)

    def copies(c, which):
        span = pl.ds(c * FETCH, FETCH)
        pairs = [(noise.at[0, span], out_u0.at[span]), (noise.at[1, span], out_u1.at[span])]
        pairs += [(mask.at[span], held_mask.at[span]), (east.at[span], held_east.at[span])]
        pairs += [(north.at[span], held_north.at[span])]
        return [pltpu.make_async_copy(*pairs[k], sem.at[c, k]) for k in which]

    fields, coefs = range(2), range(2, 5)
    for which in (coefs, fields):
        for c in range(LEVELS // FETCH):
            for copy in copies(c, which):
                copy.start()
    lane = lanes(ROWS)
    row = lax.broadcasted_iota(jnp.int32, (ROWS, COLS), 0)
    group = lane // 4

    def place(out, x, at):
        pltpu.store(out, turned(x, 4 * at + 2), mask=group == at)

    def level(l):
        k = held_mask[l].astype(F32)
        e_all = held_east[l]
        n_all = held_north[l]
        e = jnp.where(lane == COLS - 1, 0.0, e_all)
        w = jnp.where(lane == 0, 0.0, turned(e_all, 1))
        n = jnp.where(row == ROWS - 1, 0.0, n_all)
        s = jnp.where(row == 0, 0.0, slid(n_all, 1))
        for m in range(2):
            u = out_u[m][l] * k
            u_e, u_w = turned(u, -1), turned(u, 1)
            flux = e * (u_e - u) - w * (u - u_w)
            flux = flux + n * (slid(u, -1) - u) - s * (u - slid(u, 1))
            v = k * (u + flux)
            out_u[m][l] = v
            edges[m * LEVELS + l] = jnp.where(lane == COLS - 2, u_e, jnp.where(lane == 1, u_w, v))

    for c in range(LEVELS // FETCH):
        for copy in copies(c, coefs):
            copy.wait()
        for l in range(c * FETCH, (c + 1) * FETCH):
            k = held_mask[l].astype(F32)
            place(out_east, held_east[l] * k, l)
            place(out_north, held_north[l], l)
            place(out_mask, k, l)
    for c in range(LEVELS // FETCH):
        for copy in copies(c, fields):
            copy.wait()
        for l in range(c * FETCH, (c + 1) * FETCH):
            level(l)
    for g in range(2 * LEVELS):
        place(out_values, edges[g], g)
    for out in (out_east, out_north, out_mask):
        out[...] = jnp.where(lane < 64, out[...], turned(out[...], 64))


def join_rows(
    own_b, own_a, got_b, got_a, values, easts, norths, masks,
    send_2, send_1, out_values, out_east, out_north, out_mask, out_rows, south, north, side
):
    lat = lax.axis_index("lat")
    top_block = lat == lax.axis_size("lat") - 1
    even = lax.rem(lat, 2) == 0
    even_lon = lax.rem(lax.axis_index("lon"), 2) == 0

    def part(q):
        rows = pl.ds(q * LEVELS, LEVELS)
        ob, oa, gb, ga = own_b[rows, :], own_a[rows, :], got_b[rows, :], got_a[rows, :]
        return ob, oa, jnp.where(even, gb, ga), jnp.where(even, ga, gb)

    flip = COLS - 1 - lanes(LEVELS)

    def own(q):
        ob, oa, _, _ = part(q)
        back = jnp.where(top_block, jnp.take_along_axis(oa, flip, axis=1), oa)
        return jnp.where(even, ob, back), jnp.where(even, oa, ob)

    def put(ref, half, slots, x):
        for j in slots:
            ref[pl.ds(half * 64 + j, LEVELS, stride=4), :] = x

    own_n, own_k = own(4)
    _, _, far_n, far_s = part(4)
    ghost_n = jnp.where(top_block, far_n, own_n * far_n)
    for m in range(2):
        own_t, own_bot = own(m)
        _, _, up, down = part(m)
        _, _, up_p, down_p = part(2 + m)
        gain_s = own_k * far_s * (down - own_bot)
        gain_n = own_n * (up - own_t)
        out_rows[pl.ds(m * LEVELS, LEVELS), :] = gain_s
        out_rows[pl.ds((2 + m) * LEVELS, LEVELS), :] = gain_n
        out_rows[pl.ds((4 + m) * LEVELS, LEVELS), :] = down_p - far_s * (down - own_bot)
        out_rows[pl.ds((6 + m) * LEVELS, LEVELS), :] = up_p - ghost_n * (up - own_t)
        put(south, m, (0, 3), down)
        put(south, m, (1, 2), gain_s)
        put(north, m, (0, 3), up)
        put(north, m, (1, 2), gain_n)
    out_rows[pl.ds(8 * LEVELS, LEVELS), :] = far_s
    put(side, 0, (2, 3), far_s)
    tail = pl.ds(5 * LEVELS, 8)
    spread = lax.rem(lanes(8), 64) // 4
    up_e = jnp.take_along_axis(jnp.where(even, got_b[tail, :], got_a[tail, :]), spread, axis=1)
    down_e = jnp.take_along_axis(jnp.where(even, got_a[tail, :], got_b[tail, :]), spread, axis=1)

    lane1 = lanes(1)
    slot1 = lax.rem(lane1, 4)
    turned_s = jnp.transpose(south[...])
    turned_n = jnp.transpose(north[...])
    turned_c = jnp.transpose(side[...])
    row_s = jnp.where(slot1 >= 2, turned_s[0:1, :], turned_s[COLS - 1 : COLS, :])
    row_n = jnp.where(slot1 >= 2, turned_n[0:1, :], turned_n[COLS - 1 : COLS, :])
    inner = (slot1 == 1) | (slot1 == 2)
    low_half = lane1 < 64
    first_c, last_c = turned_c[0:1, :], turned_c[COLS - 1 : COLS, :]
    face_s, face_n = down_e[0:1, :], up_e[0:1, :]
    coef_s = jnp.where(slot1 == 1, turned(last_c, -1), first_c)
    coef_s = jnp.where(low_half, coef_s, turned(coef_s, 64))

    def extend(out, x, north_row, south_row):
        out[0:ROWS, :] = x[...]
        out[ROWS:PACKED, :] = jnp.zeros((PACKED - ROWS, COLS), F32)
        out[NORTH : NORTH + 1, :] = north_row
        out[SOUTH : SOUTH + 1, :] = south_row

    one = jnp.ones((1, COLS), F32)
    extend(out_values, values, row_n, row_s)
    out_values[0:1, :] = values[0:1, :] + jnp.where(inner, row_s, 0.0)
    out_values[ROWS - 1 : ROWS, :] = values[ROWS - 1 : ROWS, :] + jnp.where(inner, row_n, 0.0)
    extend(out_east, easts, jnp.where(top_block, one, face_n), face_s)
    extend(out_mask, masks, jnp.where(top_block, face_n, one), one)
    extend(out_north, norths, jnp.zeros((1, COLS), F32), coef_s)
    slot = lax.rem(lanes(PACKED), 4)
    x = out_values[...]
    eastward = jnp.where(slot >= 2, turned(x, 2), out_east[...])
    westward = jnp.where(slot < 2, turned(x, -2), out_mask[...])
    send_1[...] = jnp.where(even_lon, eastward, westward)
    send_2[...] = jnp.where(even_lon, westward, eastward)


def second_step(u1_0, u1_1, mask, east, north, rows, out):
    u1 = (u1_0, u1_1)
    lane = lanes(ROWS)
    row = lax.broadcasted_iota(jnp.int32, (ROWS, COLS), 0)

    def line(q, l):
        return rows[pl.ds(q * LEVELS + l, 1), :]

    def level(l):
        k = mask[l].astype(F32)
        e_all = east[l]
        n = north[l]
        e = jnp.where(lane == COLS - 1, 0.0, e_all)
        w = jnp.where(lane == 0, 0.0, turned(e_all, 1))
        s = jnp.where(row == 0, line(8, l), slid(n, 1))
        for m in range(2):
            u = u1[m][l]
            u = jnp.where(row == 0, u + line(m, l), u)
            u = jnp.where(row == ROWS - 1, u + line(2 + m, l), u)
            u_n = jnp.where(row == ROWS - 1, line(6 + m, l), slid(u, -1))
            u_s = jnp.where(row == 0, line(4 + m, l), slid(u, 1))
            flux = e * (turned(u, -1) - u) - w * (u - turned(u, 1))
            flux = flux + n * (u_n - u) - s * (u - u_s)
            out[m, l] = k * (u + flux)

    for l in range(LEVELS):
        level(l)


def join_columns(u2, got_2, got_1, values, easts, norths, masks, out, held, sem):
    even_lon = lax.rem(lax.axis_index("lon"), 2) == 0
    slot = lax.rem(lanes(PACKED), 4)
    is_east = slot == 1
    inner = is_east | (slot == 2)
    from_east = jnp.where(even_lon, got_1[...], got_2[...])
    from_west = jnp.where(even_lon, got_2[...], got_1[...])
    x, e, n, k = values[...], easts[...], norths[...], masks[...]
    own_0 = jnp.where(is_east, turned(x, 1), turned(x, -1))
    ghost_0 = jnp.where(is_east, from_east, from_west)
    ghost_1 = jnp.where(is_east, turned(from_east, 1), turned(from_west, -1))
    face = jnp.where(is_east, e * turned(from_east, -1), k * turned(from_west, 1))
    d = jnp.where(inner, face * (ghost_0 - own_0), 0.0)
    inside = jnp.where(is_east, turned(e, 1), e)
    s = slid(n, 1)
    change = d * (1.0 - inside - n - s) + face * (ghost_1 - x - d - d) + n * slid(d, -1) + s * slid(d, 1)
    beside = inside * d
    beside = jnp.where(slot == 0, turned(beside, -1), turned(beside, 1))
    gain = (k * jnp.where(inner, change, beside))[0:ROWS]

    lane = lanes(ROWS)
    edge = (lane < 2) | (lane >= COLS - 2)

    def copy(m, c):
        span = pl.ds(c * CHUNK, CHUNK)
        return pltpu.make_async_copy(held.at[m, span], out.at[m, span], sem.at[m, c])

    for c in range(LEVELS // CHUNK):
        for m in range(2):
            for l in range(c * CHUNK, (c + 1) * CHUNK):
                change = turned(gain, 126 - 64 * m - 4 * l)
                held[m, l] = u2[m, l] + jnp.where(edge, change, 0.0)
            copy(m, c).start()
    for c in range(LEVELS // CHUNK):
        for m in range(2):
            copy(m, c).wait()


def struct(*shape):
    return jax.ShapeDtypeStruct(shape, F32)


def kernel(body, name, inputs, outputs, us, scratch=(), space=VMEM, limit=16):
    return pl.pallas_call(
        body,
        in_specs=[space] * inputs,
        out_specs=[VMEM if body is not join_columns else HBM] * len(outputs),
        out_shape=outputs,
        scratch_shapes=list(scratch),
        compiler_params=pltpu.CompilerParams(vmem_limit_bytes=int(limit * 1024 * 1024)),
        cost_estimate=pl.CostEstimate(flops=int(us * 4e6), bytes_accessed=int(us * 3e6), transcendentals=0),
        name=name,
    )


def local(noise, land_mask, east_coef, north_coef):
    n_lat, n_lon = lax.axis_size("lat"), lax.axis_size("lon")
    message = struct(5 * LEVELS + 8, COLS)
    ends = pltpu.VMEM((2, LEVELS, 2, COLS), F32)
    scratch = [
        pltpu.VMEM((2, 2, LEVELS, 2, COLS), F32),
        pltpu.VMEM((2, LEVELS, 2, COLS), jnp.int32),
        ends,
        ends,
        pltpu.SemaphoreType.DMA((4, 2)),
    ]
    send_b, send_a = kernel(edge_rows, "edge_rows", 4, [message] * 2, 1, scratch, HBM, 53.5)(
        noise, land_mask, east_coef, north_coef
    )

    route_b = [(i, i ^ 1) for i in range(n_lat)]
    route_a = []
    for k in range(n_lon):
        for i in range(1, n_lat - 1):
            route_a.append((i * n_lon + k, (((i - 1) ^ 1) + 1) * n_lon + k))
        route_a.append(((n_lat - 1) * n_lon + k, n_lat * n_lon - 1 - k))
    got_a = lax.ppermute(send_a, ("lat", "lon"), route_a)
    got_b = lax.ppermute(send_b, "lat", route_b)

    whole, plane, packed = struct(2, LEVELS, ROWS, COLS), struct(ROWS, COLS), struct(PACKED, COLS)
    coef, levels = struct(LEVELS, ROWS, COLS), jax.ShapeDtypeStruct((LEVELS, ROWS, COLS), jnp.int32)
    outs = [coef] * 2 + [plane] * 4 + [coef] * 2 + [levels]
    scratch = [pltpu.VMEM((2 * LEVELS, ROWS, COLS), F32), pltpu.SemaphoreType.DMA((LEVELS // FETCH, 5))]
    u1_0, u1_1, *columns, east, north, mask = kernel(first_step, "first_step", 4, outs, 2, scratch, HBM, 51)(
        noise, land_mask, east_coef, north_coef
    )
    square = pltpu.VMEM((COLS, COLS), F32)
    send_2, send_1, *columns, rows = kernel(
        join_rows, "join_rows", 8, [packed] * 6 + [struct(9 * LEVELS, COLS)], 1, [square] * 3
    )(send_b, send_a, got_b, got_a, *columns)

    route_1 = [(k, k ^ 1) for k in range(n_lon)]
    route_2 = [(k, (((k + n_lon - 1) % n_lon ^ 1) + 1) % n_lon) for k in range(n_lon)]
    got_2 = lax.ppermute(send_2, "lon", route_2)
    got_1 = lax.ppermute(send_1, "lon", route_1)

    (u2,) = kernel(second_step, "second_step", 6, [whole], 2)(u1_0, u1_1, mask, east, north, rows)
    scratch = [pltpu.VMEM(whole.shape, F32), pltpu.SemaphoreType.DMA((2, LEVELS // CHUNK))]
    return kernel(join_columns, "join_columns", 7, [whole], 1, scratch)(u2, got_2, got_1, *columns)[0]


def solution(mesh):
    return jax.shard_map(
        local,
        mesh=mesh,
        in_specs=(
            P(None, None, "lat", "lon"),
            P(None, "lat", "lon"),
            P(None, "lat", "lon"),
            P(None, "lat", "lon"),
        ),
        out_specs=P(None, None, "lat", "lon"),
        check_vma=False,
    )
```
